32 devices in a mesh: grp: 4 (over y, core), blk: 8 (over z, x).
Axes of the slice: x: 2, y: 2, z: 4, core: 2. Of those that a mesh axis runs over, the one named last changes fastest.
Arguments:
- embeddings: float32 [8192, 768], P(('grp', 'blk')), may hold values from -6 to 6
- owner: int32 [8192, 1], P(('grp', 'blk')), may hold values from 0 to 3; in each aligned block of 256 rows (0 to 255, 256 to 511, ...) at most 256 rows name the same one
- cluster: int32 [8192], P(('grp', 'blk')), may hold values from 0 to 1
- order: int32 [8192], P(('grp', 'blk')), may hold values from 0 to 8191, each once
Outputs:
- nearest: float32 [8192], P(('grp', 'blk'))
The draws below stay inside these ranges and needn't reach their ends.
Inputs may be any that keep to these rules, and one draw needn't show every extreme that they name: `owner`: in the rows of one device no group is named by more than 256 rows, a bound that some block reaches.
All inputs are finite; a program needn't handle non-finite values.
Results may differ from the reference program's by a relative error of at most 0.0013.
Values may be sent and summed in bfloat16 or wider, within the bound.
A program may use at most 128 MiB of HBM per device.

```python
import math
import jax
import jax.numpy as jnp
import numpy as np
from jax import lax

D = 768
ROW_DEV = 256
CL_GRP = 2
ROWS = 8192
CAP = 256
N_GRP = 4


def set_ends(values, own_key, least, high):
    index_at = [jax.random.randint(jax.random.fold_in(own_key, axis), (), 0, length) for axis, length in enumerate(values.shape)]
    widest = values.shape.index(max(values.shape))
    beside = index_at[:widest] + [(index_at[widest] + 1) % values.shape[widest]] + index_at[widest + 1:]
    return values.at[tuple(index_at)].set(least).at[tuple(beside)].set(high)


def shard_levels(key, shape, pieces, low, top_value):
    gain, own = 1.0, jax.random.fold_in(key, 6)
    for dim, blocks in pieces:
        steps = jnp.exp(jax.random.uniform(jax.random.fold_in(own, dim), (blocks,), jnp.float32, low / len(pieces), top_value / len(pieces)))
        gain = gain * jnp.repeat(steps, shape[dim] // blocks).reshape([-1 if axis == dim else 1 for axis in range(len(shape))])
    return gain


def routed_block(own_key, own, number, rows, number_of, top, reach, slope):
    ranking = jax.random.permutation(own_key, number_of)
    heavy_load, common = shares(number_of, rows * top, reach, slope, True), shares(number_of, rows * top, reach, slope, False)
    places = jnp.arange(number_of)

    def named(sizes, rotation):
        used = int((sizes > 0).sum())
        fixed = max(1, used // 4)
        moved = fixed + (places - fixed + rotation * (used - fixed)) % max(1, number_of - fixed)
        return jnp.zeros((number_of,), jnp.int32).at[ranking[jnp.where(places < fixed, places, moved)]].set(jnp.asarray(sizes, jnp.int32))

    sizes = jnp.where(number % 4 == 0, named(heavy_load, number // 4), named(common, number - number // 4 - 1))
    mixed = jax.random.permutation(jax.random.fold_in(own, 3), number_of)
    donor, taker = mixed[0:number_of // 2 * 2:2], mixed[1:number_of // 2 * 2:2]
    slack = jnp.minimum(sizes[donor] - 1, reach - sizes[taker]) // 2
    slack = jnp.where((donor == ranking[0]) | (taker == ranking[0]) | (sizes[taker] == 0), 0, jnp.maximum(slack, 0))
    moved = jax.random.randint(jax.random.fold_in(own, 4), (number_of // 2,), 0, 1 << 20) % (slack + 1)
    sizes = sizes.at[donor].add(-moved).at[taker].add(moved)
    members = jnp.searchsorted(jnp.cumsum(sizes), jnp.arange(rows * top), side="right").astype(jnp.int32)
    table = members.reshape(top, rows).T
    table = table[jax.random.permutation(jax.random.fold_in(own, 1), rows)]
    rotation = jax.random.randint(jax.random.fold_in(own, 2), (rows, 1), 0, top)
    return jnp.take_along_axis(table, (jnp.arange(top)[None, :] + rotation) % top, axis=1)


def shares(number_of, total, bound, skew, full):
    portions = [(1 << 20) // math.isqrt(standing ** skew) + 1 for standing in range(1, number_of + 1)]
    largest = bound if full else min(bound, max(-(-total // number_of), total * portions[0] // sum(portions)))
    least = 1 if total - largest >= number_of - 1 else 0
    given, surplus = [largest] + [least] * (number_of - 1), total - largest - least * (number_of - 1)
    while surplus > 0:
        candidates = [i for i in range(1, number_of) if given[i] < largest] or [i for i in range(1, number_of) if given[i] < bound]
        mass, budget = sum([portions[i] for i in candidates]), surplus
        for i in candidates:
            extra = min(bound - given[i], max(1, budget * portions[i] // mass), surplus)
            given[i] = given[i] + extra
            surplus = surplus - extra
    return np.array(given)


def normal_values(own_key, dims, scale, bound, split=(), kind=jnp.bfloat16):
    values = jax.random.normal(own_key, dims, jnp.float32) * scale
    if len(split) > 0:
        values = shard_levels(own_key, dims, split, -0.22, 0.18) * values
    return jnp.clip(values, min=-bound, max=bound).astype(kind)


def setup_inputs(seed: int = 0) -> dict:
    streams_of = jax.random.split(jax.random.key(seed), 5)
    embeddings = normal_values(streams_of[0], (ROWS, D), 1.0, 6.0, ((0, 32),), jnp.float32)
    owner_keys = jax.random.split(jax.random.fold_in(streams_of[1], 1), ROWS // ROW_DEV)
    owner_turns = jax.random.permutation(jax.random.fold_in(streams_of[1], 3), ROWS // ROW_DEV)
    owner = jax.vmap(lambda own, number: routed_block(jax.random.fold_in(streams_of[1], 2), own, number, ROW_DEV, N_GRP, 1, CAP, 2))(owner_keys, owner_turns).reshape((ROWS, 1))
    cluster = set_ends(jax.random.randint(streams_of[2], (ROWS,), 0, CL_GRP), jax.random.fold_in(streams_of[2], 1), 0, CL_GRP - 1).astype(jnp.int32)
    order = jax.random.permutation(streams_of[3], ROWS).astype(jnp.int32)
    return {"embeddings": embeddings, "owner": owner, "cluster": cluster, "order": order}


def reference(embeddings, owner, cluster, order):
    unit = (embeddings * lax.rsqrt(lax.optimization_barrier(jnp.sum(embeddings * embeddings, axis=1, keepdims=True)) + 1e-06)).astype(jnp.bfloat16)
    ident = owner[:, 0] * CL_GRP + cluster
    block_rows = math.gcd(ROWS, 512)
    count = ROWS // block_rows

    def one_block(index):
        start = (index * block_rows).astype(jnp.int32)
        queries = lax.dynamic_slice_in_dim(unit, start, block_rows, 0)
        query_ident = lax.dynamic_slice_in_dim(ident, start, block_rows, 0)
        query_order = lax.dynamic_slice_in_dim(order, start, block_rows, 0)
        scores = lax.dot_general(queries, unit, (((1,), (1,)), ((), ())), preferred_element_type=jnp.float32)
        allowed = (query_ident[:, None] == ident[None, :]) & (order[None, :] < query_order[:, None])
        return lax.optimization_barrier(jnp.max(jnp.where(allowed, scores, jnp.float32(-1.0)), axis=1))
    nearest = lax.map(one_block, jnp.arange(count, dtype=jnp.int32))
    return nearest.reshape(ROWS)
```

```python
import functools

import jax
import jax.numpy as jnp
from jax import lax
from jax.experimental import pallas as pl
from jax.experimental.pallas import tpu as pltpu
from jax.sharding import PartitionSpec as P

MESH = pl.DeviceIdType.MESH
CHUNKS = 4


def sizes(groups, blocks):
    planes = blocks // 2
    return groups // 2, planes, groups * 2, planes // 2


def kernel(groups, blocks, emb, own_r, clu_r, ord_r, out,
           rows, line, meta_p, meta_z, row_lo, row_key, row_acc, col_acc,
           row_in, col_in, row_out,
           send, meta_recv_p, meta_recv_z, plane_recv, up_recv, down_recv,
           row_send, col_send, row_recv, col_recv):
    n = emb.shape[0]
    half, part = n // 2, n // CHUNKS
    ys, zs, ps, mid = sizes(groups, blocks)
    ups, downs = mid, zs - mid - 1
    total = n * groups * blocks
    g, b = lax.axis_index("grp"), lax.axis_index("blk")
    y, c, z, x = g // 2, g % 2, b // 2, b % 2
    x_other, c_other = 1 - x, 1 - c

    def place(x, y, c):
        return (x * ys + y) * 2 + c

    def device(x, y, c, z):
        return (y * 2 + c, z * 2 + x)

    def plane_device(p):
        return device(p // (2 * ys), (p // 2) % ys, p % 2, z)

    def y_peer(d):
        return lax.rem(y + d, ys)

    me = place(x, y, c)
    used = [0]
    started = []

    def copy(src, dst, recv, to, cond=None):
        index = used[0]
        used[0] += 1
        made = pltpu.make_async_remote_copy(
            src_ref=src, dst_ref=dst, send_sem=send.at[index], recv_sem=recv,
            device_id=to, device_id_type=MESH)
        started.append((made, cond))
        if cond is None:
            made.start()
        else:
            pl.when(cond)(made.start)

    def arrived(dst, recv):
        pltpu.make_async_remote_copy(
            src_ref=dst, dst_ref=dst, send_sem=send.at[0], recv_sem=recv,
            device_id=device(x_other, y, c, z), device_id_type=MESH).wait_recv()

    barrier = pltpu.get_barrier_semaphore()
    for d in range(1, ps):
        pl.semaphore_signal(barrier, inc=1, device_id=plane_device(lax.rem(me + d, ps)),
                            device_id_type=MESH)
    for d in range(1, zs):
        pl.semaphore_signal(barrier, inc=1, device_id=device(x, y, c, lax.rem(z + d, zs)),
                            device_id_type=MESH)

    e = emb[...]
    rows[me] = (e * lax.rsqrt(jnp.sum(e * e, axis=1, keepdims=True) + 1e-6)).astype(jnp.bfloat16)
    low = ((own_r[...] * 2 + clu_r[...]) * total).astype(jnp.float32)
    key = low + ord_r[...].astype(jnp.float32)
    first = lax.broadcasted_iota(jnp.int32, (8, n), 0) == 0
    meta = jnp.where(first, jnp.broadcast_to(low, (8, n)), jnp.broadcast_to(key, (8, n)))
    meta_p[me] = meta
    meta_z[z] = meta
    pl.semaphore_wait(barrier, ps - 1 + zs - 1)

    def piece(p, h):
        return rows.at[p, pl.ds(h * half, half)]

    def send_piece(p, h, to):
        copy(piece(p, h), piece(p, h), plane_recv.at[p, h], to)

    def wait_piece(p, h):
        arrived(piece(p, h), plane_recv.at[p, h])

    to_x, to_c = device(x_other, y, c, z), device(x, y, c_other, z)

    def slot(s, q):
        return line.at[s, pl.ds(q * part, part)]

    def own(q):
        return rows.at[me, pl.ds(q * part, part)]

    above, below = device(x, y, c, lax.rem(z + 1, zs)), device(x, y, c, lax.rem(z + zs - 1, zs))

    for d in range(1, ps):
        p = lax.rem(me + d, ps)
        copy(meta_p.at[me], meta_p.at[me], meta_recv_p.at[me], plane_device(p))
    for d in range(1, zs):
        to = device(x, y, c, lax.rem(z + d, zs))
        copy(meta_z.at[z], meta_z.at[z], meta_recv_z.at[z], to)
    for q in range(CHUNKS):
        copy(own(q), slot(0, q), up_recv.at[0, q], above, z < mid)
        if downs:
            copy(own(q), slot(ups, q), down_recv.at[0, q], below, z > mid)
    for hx, hy in ((0, 1), (1, 0)):
        send_piece(me, hx, to_x)
        for d in range(1, ys):
            send_piece(me, hy, device(x, y_peer(d), c, z))
    for h in (0, 1):
        send_piece(me, h, to_c)

    row_acc[...] = jnp.full(row_acc.shape, -1.0, jnp.float32)
    col_acc[...] = jnp.full(col_acc.shape, -1.0, jnp.float32)
    for d in range(1, ps):
        p = lax.rem(me + d, ps)
        arrived(meta_p.at[p], meta_recv_p.at[p])
    for d in range(1, zs):
        o = lax.rem(z + d, zs)
        arrived(meta_z.at[o], meta_recv_z.at[o])

    def columns(p, carry):
        m = meta_p[p]
        row_lo[p] = jnp.broadcast_to(m[0:1], (128, n)).T
        row_key[p] = jnp.broadcast_to(m[1:2], (128, n)).T
        return carry

    lax.fori_loop(0, ps, columns, 0)

    def has_up(t):
        return z > t

    def has_down(t):
        return (z >= mid) & (zs - 1 - z > t)

    def step_line(t, q):
        if t < ups:
            @pl.when(has_up(t))
            def _():
                arrived(slot(t, q), up_recv.at[t, q])
            if t + 1 < ups:
                copy(slot(t, q), slot(t + 1, q), up_recv.at[t + 1, q], above, has_up(t) & (z < mid))
            copy(slot(t, q), slot(t, q), up_recv.at[t, q], above,
                 has_up(t) & (z >= mid) & (z < zs - 1))
        if t < downs:
            @pl.when(has_down(t))
            def _():
                arrived(slot(ups + t, q), down_recv.at[t, q])
            if t + 1 < downs:
                copy(slot(ups + t, q), slot(ups + t + 1, q), down_recv.at[t + 1, q], below,
                     has_down(t) & (z > mid))

    def fold(s):
        return jnp.max(s.reshape(n // 8, 8, s.shape[1]), axis=0)

    def scores(p, block):
        return lax.dot_general(rows[p], block[...], (((1,), (1,)), ((), ())),
                               preferred_element_type=jnp.float32)

    def within_plane():
        m = meta_z[z]

        def body(p, best):
            s = scores(p, rows.at[me])
            lo, k = row_lo[p], row_key[p]
            parts = []
            for w in range(0, n, 128):
                ok = (lo == m[0:1, w:w + 128]) & (k < m[1:2, w:w + 128])
                parts.append(fold(jnp.where(ok, s[:, w:w + 128], -1.0)))
            return jnp.maximum(best, jnp.concatenate(parts, axis=1))

        col_acc[z] = lax.fori_loop(0, ps, body, jnp.full((8, n), -1.0, jnp.float32))

    def between_planes(s_index, origin):
        m = meta_z[origin]

        def body(p, best):
            s = scores(p, line.at[s_index])
            lo, k = row_lo[p], row_key[p]
            acc = row_acc[p]
            parts = []
            for w in range(0, n, 128):
                same = jnp.where(lo == m[0:1, w:w + 128], s[:, w:w + 128], -1.0)
                later = k > m[1:2, w:w + 128]
                acc = jnp.maximum(acc, jnp.where(later, same, -1.0))
                parts.append(fold(jnp.where(later, -1.0, same)))
            row_acc[p] = acc
            return jnp.maximum(best, jnp.concatenate(parts, axis=1))

        col_acc[origin] = lax.fori_loop(0, ps, body, jnp.full((8, n), -1.0, jnp.float32))

    def compute_up(t):
        @pl.when(has_up(t))
        def _():
            between_planes(t, jnp.minimum(z, mid) - 1 - t)

    def compute_down(t):
        @pl.when(has_down(t))
        def _():
            between_planes(ups + t, z + 1 + t)

    def early_plane():
        wait_piece(place(x_other, y, c), 0)
        for d in range(1, ys):
            send_piece(place(x_other, y, c), 0, device(x, y_peer(d), c, z))
        for d in range(1, ys):
            p = place(x, y_peer(d), c)
            wait_piece(p, 1)
            send_piece(p, 1, to_x)
        send_piece(place(x_other, y, c), 0, to_c)
        for d in range(1, ys):
            send_piece(place(x, y_peer(d), c), 1, to_c)

    def late_plane():
        wait_piece(place(x_other, y, c), 1)
        send_piece(place(x_other, y, c), 1, to_c)
        for d in range(1, ys):
            p = place(x, y_peer(d), c)
            wait_piece(p, 0)
            send_piece(p, 0, to_c)

    def rest_of_plane():
        for d in range(1, ys):
            p = place(x_other, y_peer(d), c)
            for h in (0, 1):
                wait_piece(p, h)
                send_piece(p, h, to_c)
        for ox in (x, x_other):
            for d in range(ys):
                for h in (0, 1):
                    wait_piece(place(ox, y_peer(d), c_other), h)

    steps = max(ups, downs)
    for t in range(steps):
        for q in range(CHUNKS):
            step_line(t, q)
            if t == 0 and q == 1:
                early_plane()
            if t == 0 and q == CHUNKS - 1:
                late_plane()
            if t == 1 and q == 1:
                rest_of_plane()
                within_plane()
            if t == 1 and q == 2:
                compute_up(0)
        if t >= 2:
            compute_up(t - 1)
            if t - 2 < downs:
                compute_down(t - 2)
    for t in range(max(0, steps - 2), downs):
        compute_down(t)
    compute_up(ups - 1)

    def go_home(p, wait):
        made = pltpu.make_async_remote_copy(
            src_ref=row_out.at[p], dst_ref=row_in.at[me], send_sem=row_send.at[p],
            recv_sem=row_recv.at[me], device_id=plane_device(p), device_id_type=MESH)
        if wait:
            made.wait_send()
        else:
            made.start()

    def line_home(o):
        return pltpu.make_async_remote_copy(
            src_ref=col_acc.at[o], dst_ref=col_in.at[z], send_sem=col_send.at[o],
            recv_sem=col_recv.at[z], device_id=device(x, y, c, o), device_id_type=MESH)

    for d in range(1, zs):
        line_home(lax.rem(z + d, zs)).start()
    for d in range(1, ps + 1):
        p = lax.rem(me + d, ps)
        t = row_acc[p].T
        row_out[p] = jnp.max(t.reshape(16, 8, n), axis=0)
        if d < ps:
            go_home(p, False)
    best = jnp.maximum(row_out[me], col_acc[z])
    for d in range(1, zs):
        o = lax.rem(z + d, zs)
        arrived(col_in.at[o], col_recv.at[o])
        best = jnp.maximum(best, col_in[o])
    for d in range(1, ps):
        p = lax.rem(me + d, ps)
        arrived(row_in.at[p], row_recv.at[p])
        best = jnp.maximum(best, row_in[p])
    out[...] = jnp.max(best, axis=0, keepdims=True)

    for made, cond in started:
        if cond is None:
            made.wait_send()
        else:
            pl.when(cond)(made.wait_send)
    for d in range(1, zs):
        line_home(lax.rem(z + d, zs)).wait_send()
    for d in range(1, ps):
        go_home(lax.rem(me + d, ps), True)


def local(embeddings, owner, cluster, order):
    groups, blocks = lax.axis_size("grp"), lax.axis_size("blk")
    n, width = embeddings.shape
    ys, zs, ps, mid = sizes(groups, blocks)
    slots = mid + max(1, zs - mid - 1)
    f32, bf16 = jnp.float32, jnp.bfloat16
    sends = (ps + zs + CHUNKS * 2 + 4 + 2 * ys + 2 + ys + 3 * ys + 2 * ys
             + 3 * CHUNKS * slots)
    dma = pltpu.SemaphoreType.DMA
    found = pl.pallas_call(
        functools.partial(kernel, groups, blocks),
        out_shape=jax.ShapeDtypeStruct((1, n), f32),
        in_specs=[pl.BlockSpec(memory_space=pltpu.VMEM)] * 4,
        out_specs=pl.BlockSpec(memory_space=pltpu.VMEM),
        scratch_shapes=[
            pltpu.VMEM((ps, n, width), bf16),
            pltpu.VMEM((slots, n, width), bf16),
            pltpu.VMEM((ps, 8, n), f32),
            pltpu.VMEM((zs, 8, n), f32),
            pltpu.VMEM((ps, n, 128), f32),
            pltpu.VMEM((ps, n, 128), f32),
            pltpu.VMEM((ps, n, 128), f32),
            pltpu.VMEM((zs, 8, n), f32),
            pltpu.VMEM((ps, 8, n), f32),
            pltpu.VMEM((zs, 8, n), f32),
            pltpu.VMEM((ps, 8, n), f32),
            dma((sends,)),
            dma((ps,)),
            dma((zs,)),
            dma((ps, 2)),
            dma((mid, CHUNKS)),
            dma((max(1, zs - mid - 1), CHUNKS)),
            dma((ps,)),
            dma((zs,)),
            dma((ps,)),
            dma((zs,)),
        ],
        compiler_params=pltpu.CompilerParams(
            collective_id=0, has_side_effects=True, vmem_limit_bytes=40 * 1024 * 1024),
    )(embeddings, owner.reshape(1, n), cluster.reshape(1, n), order.reshape(1, n))
    return found.reshape(n)


def solution(mesh):
    placed = (
        P(("grp", "blk"), None),
        P(("grp", "blk"), None),
        P(("grp", "blk")),
        P(("grp", "blk")),
    )
    return jax.shard_map(
        local, mesh=mesh, in_specs=placed, out_specs=P(("grp", "blk")), check_vma=False
    )
```

```python
import functools

import jax
import jax.numpy as jnp
from jax import lax
from jax.experimental import pallas as pl
from jax.experimental.pallas import tpu as pltpu
from jax.sharding import PartitionSpec as P

MESH = pl.DeviceIdType.MESH
CHUNKS = 4


def sizes(groups, blocks):
    planes = blocks // 2
    return groups // 2, planes, groups * 2, planes // 2


def kernel(groups, blocks, emb_h, own_h, clu_h, ord_h, out,
           emb, info, rows, line, meta_p, meta_z, col_lo, col_key, col_wide,
           row_acc, col_out, row_in, col_in,
           load, send, meta_recv_p, meta_recv_z, plane_recv, up_recv, down_recv,
           row_send, col_send, row_recv, col_recv):
    n = emb.shape[0]
    half, part = n // 2, n // CHUNKS
    ys, zs, ps, mid = sizes(groups, blocks)
    ups, downs = mid, zs - mid - 1
    total = n * groups * blocks
    g, b = lax.axis_index("grp"), lax.axis_index("blk")
    y, c, z, x = g // 2, g % 2, b // 2, b % 2
    x_other, c_other = 1 - x, 1 - c

    def place(x, y, c):
        return (x * ys + y) * 2 + c

    def device(x, y, c, z):
        return (y * 2 + c, z * 2 + x)

    def plane_device(p):
        return device(p // (2 * ys), (p // 2) % ys, p % 2, z)

    def y_peer(d):
        return lax.rem(y + d, ys)

    me = place(x, y, c)
    used = [0]
    started = []

    def copy(src, dst, recv, to, cond=None):
        index = used[0]
        used[0] += 1
        made = pltpu.make_async_remote_copy(
            src_ref=src, dst_ref=dst, send_sem=send.at[index], recv_sem=recv,
            device_id=to, device_id_type=MESH)
        started.append((made, cond))
        if cond is None:
            made.start()
        else:
            pl.when(cond)(made.start)

    def arrived(dst, recv):
        pltpu.make_async_remote_copy(
            src_ref=dst, dst_ref=dst, send_sem=send.at[0], recv_sem=recv,
            device_id=device(x_other, y, c, z), device_id_type=MESH).wait_recv()

    loads = [pltpu.make_async_copy(src, info.at[i], load.at[i])
             for i, src in enumerate((own_h, clu_h, ord_h))]
    loads += [pltpu.make_async_copy(emb_h.at[pl.ds(q * part, part)],
                                    emb.at[pl.ds(q * part, part)], load.at[3 + q])
              for q in range(CHUNKS)]
    for made in loads:
        made.start()

    barrier = pltpu.get_barrier_semaphore()
    for d in range(1, ps):
        pl.semaphore_signal(barrier, inc=1, device_id=plane_device(lax.rem(me + d, ps)),
                            device_id_type=MESH)
    for d in range(1, zs):
        pl.semaphore_signal(barrier, inc=1, device_id=device(x, y, c, lax.rem(z + d, zs)),
                            device_id_type=MESH)

    for made in loads[:3]:
        made.wait()
    low = ((info[0] * 2 + info[1]) * total).astype(jnp.float32)
    key = low + info[2].astype(jnp.float32)
    first = lax.broadcasted_iota(jnp.int32, (8, n), 0) == 0
    meta = jnp.where(first, jnp.broadcast_to(low, (8, n)), jnp.broadcast_to(key, (8, n)))
    meta_p[me] = meta
    meta_z[z] = meta
    for q in range(CHUNKS):
        loads[3 + q].wait()
        e = emb[q * part:(q + 1) * part]
        rows[me, q * part:(q + 1) * part] = (
            e * lax.rsqrt(jnp.sum(e * e, axis=1, keepdims=True) + 1e-6)).astype(jnp.bfloat16)
    pl.semaphore_wait(barrier, ps - 1 + zs - 1)

    def piece(p, h):
        return rows.at[p, pl.ds(h * half, half)]

    def send_piece(p, h, to):
        copy(piece(p, h), piece(p, h), plane_recv.at[p, h], to)

    def wait_piece(p, h):
        arrived(piece(p, h), plane_recv.at[p, h])

    to_x, to_c = device(x_other, y, c, z), device(x, y, c_other, z)

    def slot(s, q):
        return line.at[s, pl.ds(q * part, part)]

    def own(q):
        return rows.at[me, pl.ds(q * part, part)]

    above, below = device(x, y, c, lax.rem(z + 1, zs)), device(x, y, c, lax.rem(z + zs - 1, zs))

    for q in range(CHUNKS):
        copy(own(q), slot(0, q), up_recv.at[0, q], above, z < mid)
        if downs:
            copy(own(q), slot(ups, q), down_recv.at[0, q], below, z > mid)
    for hx, hy in ((0, 1), (1, 0)):
        send_piece(me, hx, to_x)
        for d in range(1, ys):
            send_piece(me, hy, device(x, y_peer(d), c, z))
    for d in range(1, ps):
        p = lax.rem(me + d, ps)
        copy(meta_p.at[me], meta_p.at[me], meta_recv_p.at[me], plane_device(p))
    for d in range(1, zs):
        to = device(x, y, c, lax.rem(z + d, zs))
        copy(meta_z.at[z], meta_z.at[z], meta_recv_z.at[z], to)
    for h in (0, 1):
        send_piece(me, h, to_c)

    def has_up(t):
        return z > t

    def has_down(t):
        return (z >= mid) & (zs - 1 - z > t)

    def step_line(t, q):
        if t < ups:
            @pl.when(has_up(t))
            def _():
                arrived(slot(t, q), up_recv.at[t, q])
            if t + 1 < ups:
                copy(slot(t, q), slot(t + 1, q), up_recv.at[t + 1, q], above, has_up(t) & (z < mid))
            copy(slot(t, q), slot(t, q), up_recv.at[t, q], above,
                 has_up(t) & (z >= mid) & (z < zs - 1))
        if t < downs:
            @pl.when(has_down(t))
            def _():
                arrived(slot(ups + t, q), down_recv.at[t, q])
            if t + 1 < downs:
                copy(slot(ups + t, q), slot(ups + t + 1, q), down_recv.at[t + 1, q], below,
                     has_down(t) & (z > mid))

    def nth(j):
        k = j // 2
        return place(lax.rem(x + k // ys, 2), lax.rem(y + k, ys), lax.rem(c + j, 2))

    near, every = (0, 2 * (ys + 1)), (0, ps)
    far = (near[1], ps)

    def fold(s):
        return jnp.max(s.reshape(s.shape[0] // 8, 8, s.shape[1]), axis=0)

    def compute(block, origin, start, count, members, both):
        span = pl.ds(start, count)

        def body(j, carry):
            p = nth(j)
            s = lax.dot_general(block[span], rows[p], (((1,), (1,)), ((), ())),
                                preferred_element_type=jnp.float32)
            lo, k, m = col_lo[origin, span], col_key[origin, span], meta_p[p]
            best = col_wide[origin, span]
            parts = []
            for w in range(0, n, 128):
                same = jnp.where(lo == m[0:1, w:w + 128], s[:, w:w + 128], -1.0)
                later = m[1:2, w:w + 128] > k
                if both:
                    best = jnp.maximum(best, jnp.where(later, -1.0, same))
                    parts.append(fold(jnp.where(later, same, -1.0)))
                else:
                    best = jnp.maximum(best, jnp.where(m[1:2, w:w + 128] < k, same, -1.0))
            col_wide[origin, span] = best
            if both:
                row_acc[p] = jnp.maximum(row_acc[p], jnp.concatenate(parts, axis=1))
            return carry

        lax.fori_loop(members[0], members[1], body, 0, unroll=2)

    def compute_own(members):
        compute(rows.at[me], z, 0, n, members, False)

    def compute_up(t, members, start=0, count=n):
        @pl.when(has_up(t))
        def _():
            compute(line.at[t], jnp.minimum(z, mid) - 1 - t, start, count, members, True)

    def compute_down(t, members):
        if t < downs:
            @pl.when(has_down(t))
            def _():
                compute(line.at[ups + t], z + 1 + t, 0, n, members, True)

    def early_plane():
        wait_piece(place(x_other, y, c), 0)
        for d in range(1, ys):
            send_piece(place(x_other, y, c), 0, device(x, y_peer(d), c, z))
        for d in range(1, ys):
            p = place(x, y_peer(d), c)
            wait_piece(p, 1)
            send_piece(p, 1, to_x)
        send_piece(place(x_other, y, c), 0, to_c)
        for d in range(1, ys):
            send_piece(place(x, y_peer(d), c), 1, to_c)

    def late_plane():
        wait_piece(place(x_other, y, c), 1)
        send_piece(place(x_other, y, c), 1, to_c)
        for d in range(1, ys):
            p = place(x, y_peer(d), c)
            wait_piece(p, 0)
            send_piece(p, 0, to_c)
        for j in range(1, near[1], 2):
            for h in (0, 1):
                wait_piece(nth(j), h)

    def far_plane():
        for d in range(1, ys):
            p = place(x_other, y_peer(d), c)
            for h in (0, 1):
                wait_piece(p, h)
                send_piece(p, h, to_c)

    def far_sibling():
        for j in range(far[0] + 1, far[1], 2):
            for h in (0, 1):
                wait_piece(nth(j), h)

    row_acc[...] = jnp.full(row_acc.shape, -1.0, jnp.float32)
    col_wide[...] = jnp.full(col_wide.shape, -1.0, jnp.float32)
    for d in range(1, zs):
        o = lax.rem(z + d, zs)
        arrived(meta_z.at[o], meta_recv_z.at[o])
    for o in range(zs):
        m = meta_z[o]
        col_lo[o] = jnp.broadcast_to(m[0:1], (128, n)).T
        col_key[o] = jnp.broadcast_to(m[1:2], (128, n)).T
    for d in range(1, ps):
        p = lax.rem(me + d, ps)
        arrived(meta_p.at[p], meta_recv_p.at[p])

    last = ups - 1
    for t in range(ups):
        for q in range(CHUNKS):
            step_line(t, q)
            if (t, q) == (0, 1):
                early_plane()
            if (t, q) == (0, CHUNKS - 1):
                late_plane()
                compute_own(near)
            if (t, q) == (1, 0):
                compute_up(0, near)
            if (t, q) == (1, 1):
                far_plane()
                compute_down(0, near)
            if (t, q) == (1, 2):
                far_sibling()
                compute_own(far)
                compute_up(0, far)
                compute_down(0, far)
            if t > 1 and q == 1:
                compute_up(t - 1, every)
                compute_down(t - 1, every)
            if (t, q) == (last, 2):
                compute_up(last, every, 0, half)

    def line_home(o):
        return pltpu.make_async_remote_copy(
            src_ref=col_out.at[o], dst_ref=col_in.at[z], send_sem=col_send.at[o],
            recv_sem=col_recv.at[z], device_id=device(x, y, c, o), device_id_type=MESH)

    def finish_line(o, cond):
        @pl.when(cond)
        def _():
            col_out[o] = fold(col_wide[o].T)
            line_home(o).start()

    def plane_home(p):
        return pltpu.make_async_remote_copy(
            src_ref=row_acc.at[p], dst_ref=row_in.at[me], send_sem=row_send.at[p],
            recv_sem=row_recv.at[me], device_id=plane_device(p), device_id_type=MESH)

    for o in range(zs):
        finish_line(o, z != o if o else (z > 0) & (z < mid))
    compute_up(last, every, half, half)
    finish_line(0, z >= mid)
    for d in range(1, ps):
        plane_home(lax.rem(me + d, ps)).start()
    best = jnp.maximum(row_acc[me], fold(col_wide[z].T))
    for d in range(1, zs):
        o = lax.rem(z + d, zs)
        arrived(col_in.at[o], col_recv.at[o])
        best = jnp.maximum(best, col_in[o])
    for d in range(1, ps):
        p = lax.rem(me + d, ps)
        arrived(row_in.at[p], row_recv.at[p])
        best = jnp.maximum(best, row_in[p])
    out[...] = jnp.max(best, axis=0, keepdims=True)

    for made, cond in started:
        if cond is None:
            made.wait_send()
        else:
            pl.when(cond)(made.wait_send)
    for d in range(1, zs):
        line_home(lax.rem(z + d, zs)).wait_send()
    for d in range(1, ps):
        plane_home(lax.rem(me + d, ps)).wait_send()


def local(embeddings, owner, cluster, order):
    groups, blocks = lax.axis_size("grp"), lax.axis_size("blk")
    n, width = embeddings.shape
    ys, zs, ps, mid = sizes(groups, blocks)
    slots = mid + max(1, zs - mid - 1)
    f32, bf16 = jnp.float32, jnp.bfloat16
    sends = (ps + zs + CHUNKS * 2 + 4 + 2 * ys + 2 + ys + 3 * ys + 2 * ys
             + 3 * CHUNKS * slots)
    dma = pltpu.SemaphoreType.DMA
    found = pl.pallas_call(
        functools.partial(kernel, groups, blocks),
        out_shape=jax.ShapeDtypeStruct((1, n), f32),
        in_specs=[pl.BlockSpec(memory_space=pltpu.HBM)] * 4,
        out_specs=pl.BlockSpec(memory_space=pltpu.VMEM),
        scratch_shapes=[
            pltpu.VMEM((n, width), f32),
            pltpu.VMEM((3, 1, n), jnp.int32),
            pltpu.VMEM((ps, n, width), bf16),
            pltpu.VMEM((slots, n, width), bf16),
            pltpu.VMEM((ps, 8, n), f32),
            pltpu.VMEM((zs, 8, n), f32),
            pltpu.VMEM((zs, n, 128), f32),
            pltpu.VMEM((zs, n, 128), f32),
            pltpu.VMEM((zs, n, 128), f32),
            pltpu.VMEM((ps, 8, n), f32),
            pltpu.VMEM((zs, 8, n), f32),
            pltpu.VMEM((ps, 8, n), f32),
            pltpu.VMEM((zs, 8, n), f32),
            dma((3 + CHUNKS,)),
            dma((sends,)),
            dma((ps,)),
            dma((zs,)),
            dma((ps, 2)),
            dma((mid, CHUNKS)),
            dma((max(1, zs - mid - 1), CHUNKS)),
            dma((ps,)),
            dma((zs,)),
            dma((ps,)),
            dma((zs,)),
        ],
        compiler_params=pltpu.CompilerParams(
            collective_id=0, has_side_effects=True, vmem_limit_bytes=64 * 1024 * 1024 - 524288),
    )(embeddings, owner.reshape(1, n), cluster.reshape(1, n), order.reshape(1, n))
    return found.reshape(n)


def solution(mesh):
    placed = (
        P(("grp", "blk"), None),
        P(("grp", "blk"), None),
        P(("grp", "blk")),
        P(("grp", "blk")),
    )
    return jax.shard_map(
        local, mesh=mesh, in_specs=placed, out_specs=P(("grp", "blk")), check_vma=False
    )
```

```python
import functools

import jax
import jax.numpy as jnp
from jax import lax
from jax.experimental import pallas as pl
from jax.experimental.pallas import tpu as pltpu
from jax.sharding import PartitionSpec as P

MESH = pl.DeviceIdType.MESH
CHUNKS = 4


def sizes(groups, blocks):
    planes = blocks // 2
    return groups // 2, planes, groups * 2, planes // 2


def kernel(groups, blocks, emb_h, own_h, clu_h, ord_h, out,
           emb, info, rows, line, meta_p, meta_z, col_lo, col_key, col_wide,
           row_acc, col_out, row_in, col_in,
           load, send, meta_recv_p, meta_recv_z, plane_recv, up_recv, down_recv,
           row_send, col_send, row_recv, col_recv):
    n = emb.shape[0]
    half, part = n // 2, n // CHUNKS
    ys, zs, ps, mid = sizes(groups, blocks)
    ups, downs = mid, zs - mid - 1
    total = n * groups * blocks
    g, b = lax.axis_index("grp"), lax.axis_index("blk")
    y, c, z, x = g // 2, g % 2, b // 2, b % 2
    x_other, c_other = 1 - x, 1 - c

    def place(x, y, c):
        return (x * ys + y) * 2 + c

    def device(x, y, c, z):
        return (y * 2 + c, z * 2 + x)

    def plane_device(p):
        return device(p // (2 * ys), (p // 2) % ys, p % 2, z)

    def y_peer(d):
        return lax.rem(y + d, ys)

    me = place(x, y, c)
    used = [0]
    started = []

    def copy(src, dst, recv, to, cond=None):
        index = used[0]
        used[0] += 1
        made = pltpu.make_async_remote_copy(
            src_ref=src, dst_ref=dst, send_sem=send.at[index], recv_sem=recv,
            device_id=to, device_id_type=MESH)
        started.append((made, cond))
        if cond is None:
            made.start()
        else:
            pl.when(cond)(made.start)

    def arrived(dst, recv):
        pltpu.make_async_remote_copy(
            src_ref=dst, dst_ref=dst, send_sem=send.at[0], recv_sem=recv,
            device_id=device(x_other, y, c, z), device_id_type=MESH).wait_recv()

    loads = [pltpu.make_async_copy(src, info.at[i], load.at[i])
             for i, src in enumerate((own_h, clu_h, ord_h))]
    loads += [pltpu.make_async_copy(emb_h.at[pl.ds(q * part, part)],
                                    emb.at[pl.ds(q * part, part)], load.at[3 + q])
              for q in range(CHUNKS)]
    for made in loads:
        made.start()

    barrier = pltpu.get_barrier_semaphore()
    for d in range(1, ps):
        pl.semaphore_signal(barrier, inc=1, device_id=plane_device(lax.rem(me + d, ps)),
                            device_id_type=MESH)
    for d in range(1, zs):
        pl.semaphore_signal(barrier, inc=1, device_id=device(x, y, c, lax.rem(z + d, zs)),
                            device_id_type=MESH)

    for made in loads[:3]:
        made.wait()
    low = ((info[0] * 2 + info[1]) * total).astype(jnp.float32)
    key = low + info[2].astype(jnp.float32)
    first = lax.broadcasted_iota(jnp.int32, (8, n), 0) == 0
    meta = jnp.where(first, jnp.broadcast_to(low, (8, n)), jnp.broadcast_to(key, (8, n)))
    meta_p[me] = meta
    meta_z[z] = meta
    for q in range(CHUNKS):
        loads[3 + q].wait()
        e = emb[q * part:(q + 1) * part]
        rows[me, q * part:(q + 1) * part] = (
            e * lax.rsqrt(jnp.sum(e * e, axis=1, keepdims=True) + 1e-6)).astype(jnp.bfloat16)
    pl.semaphore_wait(barrier, ps - 1 + zs - 1)

    def piece(p, h):
        return rows.at[p, pl.ds(h * half, half)]

    def send_piece(p, h, to):
        copy(piece(p, h), piece(p, h), plane_recv.at[p, h], to)

    def wait_piece(p, h):
        arrived(piece(p, h), plane_recv.at[p, h])

    to_x, to_c = device(x_other, y, c, z), device(x, y, c_other, z)

    def slot(s, q):
        return line.at[s, pl.ds(q * part, part)]

    def own(q):
        return rows.at[me, pl.ds(q * part, part)]

    above, below = device(x, y, c, lax.rem(z + 1, zs)), device(x, y, c, lax.rem(z + zs - 1, zs))

    for d in range(1, ps):
        p = lax.rem(me + d, ps)
        copy(meta_p.at[me], meta_p.at[me], meta_recv_p.at[me], plane_device(p))
    for d in range(1, zs):
        to = device(x, y, c, lax.rem(z + d, zs))
        copy(meta_z.at[z], meta_z.at[z], meta_recv_z.at[z], to)
    for q in range(CHUNKS):
        copy(own(q), slot(0, q), up_recv.at[0, q], above, z < mid)
        if downs:
            copy(own(q), slot(ups, q), down_recv.at[0, q], below, z > mid)
    for hx, hy in ((0, 1), (1, 0)):
        send_piece(me, hx, to_x)
        for d in range(1, ys):
            send_piece(me, hy, device(x, y_peer(d), c, z))
    for h in (0, 1):
        send_piece(me, h, to_c)

    def has_up(t):
        return z > t

    def has_down(t):
        return (z >= mid) & (zs - 1 - z > t)

    def step_line(t, q):
        if t < ups:
            @pl.when(has_up(t))
            def _():
                arrived(slot(t, q), up_recv.at[t, q])
            if t + 1 < ups:
                copy(slot(t, q), slot(t + 1, q), up_recv.at[t + 1, q], above, has_up(t) & (z < mid))
            copy(slot(t, q), slot(t, q), up_recv.at[t, q], above,
                 has_up(t) & (z >= mid) & (z < zs - 1))
        if t < downs:
            @pl.when(has_down(t))
            def _():
                arrived(slot(ups + t, q), down_recv.at[t, q])
            if t + 1 < downs:
                copy(slot(ups + t, q), slot(ups + t + 1, q), down_recv.at[t + 1, q], below,
                     has_down(t) & (z > mid))

    def nth(j):
        k = j // 2
        return place(lax.rem(x + k // ys, 2), lax.rem(y + k, ys), lax.rem(c + j, 2))

    near, every = (0, 2 * (ys + 1)), (0, ps)
    far = (near[1], ps)

    def fold(s):
        return jnp.max(s.reshape(s.shape[0] // 8, 8, s.shape[1]), axis=0)

    def compute(block, origin, start, count, members, both):
        span = pl.ds(start, count)

        def body(j, carry):
            p = nth(j)
            s = lax.dot_general(block[span], rows[p], (((1,), (1,)), ((), ())),
                                preferred_element_type=jnp.float32)
            lo, k, m = col_lo[origin, span], col_key[origin, span], meta_p[p]
            best = col_wide[origin, span]
            parts = []
            for w in range(0, n, 128):
                same = jnp.where(lo == m[0:1, w:w + 128], s[:, w:w + 128], -1.0)
                later = m[1:2, w:w + 128] > k
                if both:
                    best = jnp.maximum(best, jnp.where(later, -1.0, same))
                    parts.append(fold(jnp.where(later, same, -1.0)))
                else:
                    best = jnp.maximum(best, jnp.where(m[1:2, w:w + 128] < k, same, -1.0))
            col_wide[origin, span] = best
            if both:
                row_acc[p] = jnp.maximum(row_acc[p], jnp.concatenate(parts, axis=1))
            return carry

        lax.fori_loop(members[0], members[1], body, 0, unroll=2)

    def compute_own(members):
        compute(rows.at[me], z, 0, n, members, False)

    def compute_up(t, members, start=0, count=n):
        @pl.when(has_up(t))
        def _():
            compute(line.at[t], jnp.minimum(z, mid) - 1 - t, start, count, members, True)

    def compute_down(t, members):
        if t < downs:
            @pl.when(has_down(t))
            def _():
                compute(line.at[ups + t], z + 1 + t, 0, n, members, True)

    def early_plane():
        wait_piece(place(x_other, y, c), 0)
        for d in range(1, ys):
            send_piece(place(x_other, y, c), 0, device(x, y_peer(d), c, z))
        for d in range(1, ys):
            p = place(x, y_peer(d), c)
            wait_piece(p, 1)
            send_piece(p, 1, to_x)
        send_piece(place(x_other, y, c), 0, to_c)
        for d in range(1, ys):
            send_piece(place(x, y_peer(d), c), 1, to_c)

    def late_plane():
        wait_piece(place(x_other, y, c), 1)
        send_piece(place(x_other, y, c), 1, to_c)
        for d in range(1, ys):
            p = place(x, y_peer(d), c)
            wait_piece(p, 0)
            send_piece(p, 0, to_c)
        for j in range(1, near[1], 2):
            for h in (0, 1):
                wait_piece(nth(j), h)

    def far_plane():
        for d in range(1, ys):
            p = place(x_other, y_peer(d), c)
            for h in (0, 1):
                wait_piece(p, h)
                send_piece(p, h, to_c)

    def far_sibling():
        for j in range(far[0] + 1, far[1], 2):
            for h in (0, 1):
                wait_piece(nth(j), h)

    row_acc[...] = jnp.full(row_acc.shape, -1.0, jnp.float32)
    col_wide[...] = jnp.full(col_wide.shape, -1.0, jnp.float32)

    def keys():
        for d in range(1, ps):
            p = lax.rem(me + d, ps)
            arrived(meta_p.at[p], meta_recv_p.at[p])
        for d in range(1, zs):
            o = lax.rem(z + d, zs)
            arrived(meta_z.at[o], meta_recv_z.at[o])
        for o in range(zs):
            m = meta_z[o]
            col_lo[o] = jnp.broadcast_to(m[0:1], (128, n)).T
            col_key[o] = jnp.broadcast_to(m[1:2], (128, n)).T

    last = ups - 1
    for t in range(ups):
        for q in range(CHUNKS):
            step_line(t, q)
            if (t, q) == (0, 1):
                early_plane()
                keys()
            if (t, q) == (0, CHUNKS - 1):
                late_plane()
                compute_own(near)
            if (t, q) == (1, 0):
                compute_up(0, near)
            if (t, q) == (1, 1):
                far_plane()
                compute_down(0, near)
            if (t, q) == (1, 2):
                far_sibling()
                compute_own(far)
                compute_up(0, far)
                compute_down(0, far)
            if t > 1 and q == 1:
                compute_up(t - 1, every)
                compute_down(t - 1, every)
            if (t, q) == (last, 2):
                compute_up(last, every, 0, half)

    def line_home(o):
        return pltpu.make_async_remote_copy(
            src_ref=col_out.at[o], dst_ref=col_in.at[z], send_sem=col_send.at[o],
            recv_sem=col_recv.at[z], device_id=device(x, y, c, o), device_id_type=MESH)

    def finish_line(o, cond):
        @pl.when(cond)
        def _():
            col_out[o] = fold(col_wide[o].T)
            line_home(o).start()

    def plane_home(p):
        return pltpu.make_async_remote_copy(
            src_ref=row_acc.at[p], dst_ref=row_in.at[me], send_sem=row_send.at[p],
            recv_sem=row_recv.at[me], device_id=plane_device(p), device_id_type=MESH)

    for o in range(zs):
        finish_line(o, z != o if o else (z > 0) & (z < mid))
    compute_up(last, every, half, half)
    finish_line(0, z >= mid)
    for d in range(1, ps):
        plane_home(lax.rem(me + d, ps)).start()
    best = jnp.maximum(row_acc[me], fold(col_wide[z].T))
    for d in range(1, zs):
        o = lax.rem(z + d, zs)
        arrived(col_in.at[o], col_recv.at[o])
        best = jnp.maximum(best, col_in[o])
    for d in range(1, ps):
        p = lax.rem(me + d, ps)
        arrived(row_in.at[p], row_recv.at[p])
        best = jnp.maximum(best, row_in[p])
    out[...] = jnp.max(best, axis=0, keepdims=True)

    for made, cond in started:
        if cond is None:
            made.wait_send()
        else:
            pl.when(cond)(made.wait_send)
    for d in range(1, zs):
        line_home(lax.rem(z + d, zs)).wait_send()
    for d in range(1, ps):
        plane_home(lax.rem(me + d, ps)).wait_send()


def local(embeddings, owner, cluster, order):
    groups, blocks = lax.axis_size("grp"), lax.axis_size("blk")
    n, width = embeddings.shape
    ys, zs, ps, mid = sizes(groups, blocks)
    slots = mid + max(1, zs - mid - 1)
    f32, bf16 = jnp.float32, jnp.bfloat16
    sends = (ps + zs + CHUNKS * 2 + 4 + 2 * ys + 2 + ys + 3 * ys + 2 * ys
             + 3 * CHUNKS * slots)
    dma = pltpu.SemaphoreType.DMA
    found = pl.pallas_call(
        functools.partial(kernel, groups, blocks),
        out_shape=jax.ShapeDtypeStruct((1, n), f32),
        in_specs=[pl.BlockSpec(memory_space=pltpu.HBM)] * 4,
        out_specs=pl.BlockSpec(memory_space=pltpu.VMEM),
        scratch_shapes=[
            pltpu.VMEM((n, width), f32),
            pltpu.VMEM((3, 1, n), jnp.int32),
            pltpu.VMEM((ps, n, width), bf16),
            pltpu.VMEM((slots, n, width), bf16),
            pltpu.VMEM((ps, 8, n), f32),
            pltpu.VMEM((zs, 8, n), f32),
            pltpu.VMEM((zs, n, 128), f32),
            pltpu.VMEM((zs, n, 128), f32),
            pltpu.VMEM((zs, n, 128), f32),
            pltpu.VMEM((ps, 8, n), f32),
            pltpu.VMEM((zs, 8, n), f32),
            pltpu.VMEM((ps, 8, n), f32),
            pltpu.VMEM((zs, 8, n), f32),
            dma((3 + CHUNKS,)),
            dma((sends,)),
            dma((ps,)),
            dma((zs,)),
            dma((ps, 2)),
            dma((mid, CHUNKS)),
            dma((max(1, zs - mid - 1), CHUNKS)),
            dma((ps,)),
            dma((zs,)),
            dma((ps,)),
            dma((zs,)),
        ],
        compiler_params=pltpu.CompilerParams(
            collective_id=0, has_side_effects=True, vmem_limit_bytes=64 * 1024 * 1024 - 524288),
    )(embeddings, owner.reshape(1, n), cluster.reshape(1, n), order.reshape(1, n))
    return found.reshape(n)


def solution(mesh):
    placed = (
        P(("grp", "blk"), None),
        P(("grp", "blk"), None),
        P(("grp", "blk")),
        P(("grp", "blk")),
    )
    return jax.shard_map(
        local, mesh=mesh, in_specs=placed, out_specs=P(("grp", "blk")), check_vma=False
    )
```

```python
import functools

import jax
import jax.numpy as jnp
from jax import lax
from jax.experimental import pallas as pl
from jax.experimental.pallas import tpu as pltpu
from jax.sharding import PartitionSpec as P

MESH = pl.DeviceIdType.MESH
CHUNKS = 4


def sizes(groups, blocks):
    planes = blocks // 2
    return groups // 2, planes, groups * 2, planes // 2


def kernel(groups, blocks, emb_h, own_h, clu_h, ord_h, out,
           emb, info, rows, line, meta_p, meta_z, col_lo, col_key, col_wide,
           row_acc, col_out, row_in, col_in,
           load, send, meta_recv_p, meta_recv_z, plane_recv, up_recv, down_recv,
           row_send, col_send, row_recv, col_recv):
    n = emb.shape[0]
    half, part = n // 2, n // CHUNKS
    ys, zs, ps, mid = sizes(groups, blocks)
    ups, downs = mid, zs - mid - 1
    total = n * groups * blocks
    g, b = lax.axis_index("grp"), lax.axis_index("blk")
    y, c, z, x = g // 2, g % 2, b // 2, b % 2
    x_other, c_other = 1 - x, 1 - c

    def place(x, y, c):
        return (x * ys + y) * 2 + c

    def device(x, y, c, z):
        return (y * 2 + c, z * 2 + x)

    def plane_device(p):
        return device(p // (2 * ys), (p // 2) % ys, p % 2, z)

    def y_peer(d):
        return lax.rem(y + d, ys)

    me = place(x, y, c)
    used = [0]
    started = []

    def copy(src, dst, recv, to, cond=None):
        index = used[0]
        used[0] += 1
        made = pltpu.make_async_remote_copy(
            src_ref=src, dst_ref=dst, send_sem=send.at[index], recv_sem=recv,
            device_id=to, device_id_type=MESH)
        started.append((made, cond))
        if cond is None:
            made.start()
        else:
            pl.when(cond)(made.start)

    def arrived(dst, recv):
        pltpu.make_async_remote_copy(
            src_ref=dst, dst_ref=dst, send_sem=send.at[0], recv_sem=recv,
            device_id=device(x_other, y, c, z), device_id_type=MESH).wait_recv()

    loads = [pltpu.make_async_copy(src, info.at[i], load.at[i])
             for i, src in enumerate((own_h, clu_h, ord_h))]
    loads += [pltpu.make_async_copy(emb_h.at[pl.ds(q * part, part)],
                                    emb.at[pl.ds(q * part, part)], load.at[3 + q])
              for q in range(CHUNKS)]
    for made in loads:
        made.start()

    barrier = pltpu.get_barrier_semaphore()
    for d in range(1, ps):
        pl.semaphore_signal(barrier, inc=1, device_id=plane_device(lax.rem(me + d, ps)),
                            device_id_type=MESH)
    for d in range(1, zs):
        pl.semaphore_signal(barrier, inc=1, device_id=device(x, y, c, lax.rem(z + d, zs)),
                            device_id_type=MESH)

    for made in loads[:3]:
        made.wait()
    low = ((info[0] * 2 + info[1]) * total).astype(jnp.float32)
    key = low + info[2].astype(jnp.float32)
    first = lax.broadcasted_iota(jnp.int32, (8, n), 0) == 0
    meta = jnp.where(first, jnp.broadcast_to(low, (8, n)), jnp.broadcast_to(key, (8, n)))
    meta_p[me] = meta
    meta_z[z] = meta
    for q in range(CHUNKS):
        loads[3 + q].wait()
        e = emb[q * part:(q + 1) * part]
        rows[me, q * part:(q + 1) * part] = (
            e * lax.rsqrt(jnp.sum(e * e, axis=1, keepdims=True) + 1e-6)).astype(jnp.bfloat16)
    pl.semaphore_wait(barrier, ps - 1 + zs - 1)

    def piece(p, h):
        return rows.at[p, pl.ds(h * half, half)]

    def send_piece(p, h, to):
        copy(piece(p, h), piece(p, h), plane_recv.at[p, h], to)

    def wait_piece(p, h):
        arrived(piece(p, h), plane_recv.at[p, h])

    to_x, to_c = device(x_other, y, c, z), device(x, y, c_other, z)

    def slot(s, q):
        return line.at[s, pl.ds(q * part, part)]

    def own(q):
        return rows.at[me, pl.ds(q * part, part)]

    above, below = device(x, y, c, lax.rem(z + 1, zs)), device(x, y, c, lax.rem(z + zs - 1, zs))

    for d in range(1, ps):
        p = lax.rem(me + d, ps)
        copy(meta_p.at[me], meta_p.at[me], meta_recv_p.at[me], plane_device(p))
    for d in range(1, zs):
        to = device(x, y, c, lax.rem(z + d, zs))
        copy(meta_z.at[z], meta_z.at[z], meta_recv_z.at[z], to)
    for q in range(CHUNKS):
        copy(own(q), slot(0, q), up_recv.at[0, q], above, z < mid)
        if downs:
            copy(own(q), slot(ups, q), down_recv.at[0, q], below, z >= mid)
    for hx, hy in ((0, 1), (1, 0)):
        send_piece(me, hx, to_x)
        for d in range(1, ys):
            send_piece(me, hy, device(x, y_peer(d), c, z))
    for h in (0, 1):
        send_piece(me, h, to_c)

    def has_up(t):
        return z > t

    def has_down(t):
        return (z < mid) | (zs - 1 - z > t)

    def step_line(t, q):
        if t < ups:
            @pl.when(has_up(t))
            def _():
                arrived(slot(t, q), up_recv.at[t, q])
            if t + 1 < ups:
                copy(slot(t, q), slot(t + 1, q), up_recv.at[t + 1, q], above, has_up(t) & (z < mid))
            copy(slot(t, q), slot(t, q), up_recv.at[t, q], above,
                 has_up(t) & (z >= mid) & (z < zs - 1))
        if t < downs:
            @pl.when(has_down(t))
            def _():
                arrived(slot(ups + t, q), down_recv.at[t, q])
            if t + 1 < downs:
                copy(slot(ups + t, q), slot(ups + t + 1, q), down_recv.at[t + 1, q], below,
                     has_down(t) & (z >= mid))
            copy(slot(ups + t, q), slot(ups + t, q), down_recv.at[t, q], below, (z > 0) & (z < mid))

    def nth(j):
        k = j // 2
        return place(lax.rem(x + k // ys, 2), lax.rem(y + k, ys), lax.rem(c + j, 2))

    near, every = (0, 2 * (ys + 1)), (0, ps)
    far = (near[1], ps)

    def fold(s):
        return jnp.max(s.reshape(s.shape[0] // 8, 8, s.shape[1]), axis=0)

    def compute(block, origin, start, count, members, both):
        span = pl.ds(start, count)

        def body(j, carry):
            p = nth(j)
            s = lax.dot_general(block[span], rows[p], (((1,), (1,)), ((), ())),
                                preferred_element_type=jnp.float32)
            lo, k, m = col_lo[origin, span], col_key[origin, span], meta_p[p]
            best = col_wide[origin, span]
            parts = []
            for w in range(0, n, 128):
                same = jnp.where(lo == m[0:1, w:w + 128], s[:, w:w + 128], -1.0)
                later = m[1:2, w:w + 128] > k
                if both:
                    best = jnp.maximum(best, jnp.where(later, -1.0, same))
                    parts.append(fold(jnp.where(later, same, -1.0)))
                else:
                    best = jnp.maximum(best, jnp.where(m[1:2, w:w + 128] < k, same, -1.0))
            col_wide[origin, span] = best
            if both:
                row_acc[p] = jnp.maximum(row_acc[p], jnp.concatenate(parts, axis=1))
            return carry

        lax.fori_loop(members[0], members[1], body, 0, unroll=2)

    def compute_own(members):
        compute(rows.at[me], z, 0, n, members, False)

    def compute_up(t, members, start=0, count=n):
        @pl.when(has_up(t) & ((z < mid) | (z == zs - 1)))
        def _():
            compute(line.at[t], jnp.minimum(z, mid) - 1 - t, start, count, members, True)

    def compute_down(t, members):
        if t < downs:
            @pl.when(has_down(t))
            def _():
                compute(line.at[ups + t], jnp.maximum(z + 1, mid) + t, 0, n, members, True)

    def early_plane():
        wait_piece(place(x_other, y, c), 0)
        for d in range(1, ys):
            send_piece(place(x_other, y, c), 0, device(x, y_peer(d), c, z))
        for d in range(1, ys):
            p = place(x, y_peer(d), c)
            wait_piece(p, 1)
            send_piece(p, 1, to_x)
        send_piece(place(x_other, y, c), 0, to_c)
        for d in range(1, ys):
            send_piece(place(x, y_peer(d), c), 1, to_c)

    def late_plane():
        wait_piece(place(x_other, y, c), 1)
        send_piece(place(x_other, y, c), 1, to_c)
        for d in range(1, ys):
            p = place(x, y_peer(d), c)
            wait_piece(p, 0)
            send_piece(p, 0, to_c)
        for j in range(1, near[1], 2):
            for h in (0, 1):
                wait_piece(nth(j), h)

    def far_plane():
        for d in range(1, ys):
            p = place(x_other, y_peer(d), c)
            for h in (0, 1):
                wait_piece(p, h)
                send_piece(p, h, to_c)

    def far_sibling():
        for j in range(far[0] + 1, far[1], 2):
            for h in (0, 1):
                wait_piece(nth(j), h)

    row_acc[...] = jnp.full(row_acc.shape, -1.0, jnp.float32)
    col_wide[...] = jnp.full(col_wide.shape, -1.0, jnp.float32)

    def keys():
        for d in range(1, ps):
            p = lax.rem(me + d, ps)
            arrived(meta_p.at[p], meta_recv_p.at[p])
        for d in range(1, zs):
            o = lax.rem(z + d, zs)
            arrived(meta_z.at[o], meta_recv_z.at[o])
        for o in range(zs):
            m = meta_z[o]
            col_lo[o] = jnp.broadcast_to(m[0:1], (128, n)).T
            col_key[o] = jnp.broadcast_to(m[1:2], (128, n)).T

    last = ups - 1
    for t in range(ups):
        for q in range(CHUNKS):
            step_line(t, q)
            if (t, q) == (0, 1):
                early_plane()
                keys()
            if (t, q) == (0, CHUNKS - 1):
                late_plane()
                compute_own(near)
            if (t, q) == (1, 0):
                compute_up(0, near)
            if (t, q) == (1, 1):
                far_plane()
                compute_down(0, near)
            if (t, q) == (1, 2):
                far_sibling()
                compute_own(far)
                compute_up(0, far)
                compute_down(0, far)
            if t > 1 and q == 1:
                compute_up(t - 1, every)
                compute_down(t - 1, every)
            if (t, q) == (last, 2):
                compute_up(last, every, 0, half)

    def line_home(o):
        return pltpu.make_async_remote_copy(
            src_ref=col_out.at[o], dst_ref=col_in.at[z], send_sem=col_send.at[o],
            recv_sem=col_recv.at[z], device_id=device(x, y, c, o), device_id_type=MESH)

    def finish_line(o, cond):
        @pl.when(cond)
        def _():
            col_out[o] = fold(col_wide[o].T)
            line_home(o).start()

    def plane_home(p):
        return pltpu.make_async_remote_copy(
            src_ref=row_acc.at[p], dst_ref=row_in.at[me], send_sem=row_send.at[p],
            recv_sem=row_recv.at[me], device_id=plane_device(p), device_id_type=MESH)

    for o in range(zs):
        finish_line(o, z != o if o else (z > 0) & (z < zs - 1))
    compute_up(last, every, half, half)
    finish_line(0, z == zs - 1)
    for d in range(1, ps):
        plane_home(lax.rem(me + d, ps)).start()
    best = jnp.maximum(row_acc[me], fold(col_wide[z].T))
    for d in range(1, zs):
        o = lax.rem(z + d, zs)
        arrived(col_in.at[o], col_recv.at[o])
        best = jnp.maximum(best, col_in[o])
    for d in range(1, ps):
        p = lax.rem(me + d, ps)
        arrived(row_in.at[p], row_recv.at[p])
        best = jnp.maximum(best, row_in[p])
    out[...] = jnp.max(best, axis=0, keepdims=True)

    for made, cond in started:
        if cond is None:
            made.wait_send()
        else:
            pl.when(cond)(made.wait_send)
    for d in range(1, zs):
        line_home(lax.rem(z + d, zs)).wait_send()
    for d in range(1, ps):
        plane_home(lax.rem(me + d, ps)).wait_send()


def local(embeddings, owner, cluster, order):
    groups, blocks = lax.axis_size("grp"), lax.axis_size("blk")
    n, width = embeddings.shape
    ys, zs, ps, mid = sizes(groups, blocks)
    slots = mid + max(1, zs - mid - 1)
    f32, bf16 = jnp.float32, jnp.bfloat16
    sends = (ps + zs + CHUNKS * 2 + 4 + 2 * ys + 2 + ys + 3 * ys + 2 * ys
             + 4 * CHUNKS * slots)
    dma = pltpu.SemaphoreType.DMA
    found = pl.pallas_call(
        functools.partial(kernel, groups, blocks),
        out_shape=jax.ShapeDtypeStruct((1, n), f32),
        in_specs=[pl.BlockSpec(memory_space=pltpu.HBM)] * 4,
        out_specs=pl.BlockSpec(memory_space=pltpu.VMEM),
        scratch_shapes=[
            pltpu.VMEM((n, width), f32),
            pltpu.VMEM((3, 1, n), jnp.int32),
            pltpu.VMEM((ps, n, width), bf16),
            pltpu.VMEM((slots, n, width), bf16),
            pltpu.VMEM((ps, 8, n), f32),
            pltpu.VMEM((zs, 8, n), f32),
            pltpu.VMEM((zs, n, 128), f32),
            pltpu.VMEM((zs, n, 128), f32),
            pltpu.VMEM((zs, n, 128), f32),
            pltpu.VMEM((ps, 8, n), f32),
            pltpu.VMEM((zs, 8, n), f32),
            pltpu.VMEM((ps, 8, n), f32),
            pltpu.VMEM((zs, 8, n), f32),
            dma((3 + CHUNKS,)),
            dma((sends,)),
            dma((ps,)),
            dma((zs,)),
            dma((ps, 2)),
            dma((mid, CHUNKS)),
            dma((max(1, zs - mid - 1), CHUNKS)),
            dma((ps,)),
            dma((zs,)),
            dma((ps,)),
            dma((zs,)),
        ],
        compiler_params=pltpu.CompilerParams(
            collective_id=0, has_side_effects=True, vmem_limit_bytes=64 * 1024 * 1024 - 524288),
    )(embeddings, owner.reshape(1, n), cluster.reshape(1, n), order.reshape(1, n))
    return found.reshape(n)


def solution(mesh):
    placed = (
        P(("grp", "blk"), None),
        P(("grp", "blk"), None),
        P(("grp", "blk")),
        P(("grp", "blk")),
    )
    return jax.shard_map(
        local, mesh=mesh, in_specs=placed, out_specs=P(("grp", "blk")), check_vma=False
    )
```

```python
import functools

import jax
import jax.numpy as jnp
from jax import lax
from jax.experimental import pallas as pl
from jax.experimental.pallas import tpu as pltpu
from jax.sharding import PartitionSpec as P

MESH = pl.DeviceIdType.MESH
CHUNKS = 4


def sizes(groups, blocks):
    planes = blocks // 2
    return groups // 2, planes, groups * 2, planes // 2


def kernel(groups, blocks, emb_h, own_h, clu_h, ord_h, out,
           emb, info, rows, line, meta_p, meta_z, col_lo, col_key, col_wide,
           row_acc, col_out, row_in, col_in,
           load, send, meta_recv_p, meta_recv_z, plane_recv, up_recv, down_recv,
           row_send, col_send, row_recv, col_recv):
    n = emb.shape[0]
    half, part = n // 2, n // CHUNKS
    ys, zs, ps, mid = sizes(groups, blocks)
    ups, downs = mid, zs - mid - 1
    total = n * groups * blocks
    g, b = lax.axis_index("grp"), lax.axis_index("blk")
    y, c, z, x = g // 2, g % 2, b // 2, b % 2
    x_other, c_other = 1 - x, 1 - c

    def place(x, y, c):
        return (x * ys + y) * 2 + c

    def device(x, y, c, z):
        return (y * 2 + c, z * 2 + x)

    def plane_device(p):
        return device(p // (2 * ys), (p // 2) % ys, p % 2, z)

    def y_peer(d):
        return lax.rem(y + d, ys)

    me = place(x, y, c)
    used = [0]
    started = []

    def copy(src, dst, recv, to, cond=None):
        index = used[0]
        used[0] += 1
        made = pltpu.make_async_remote_copy(
            src_ref=src, dst_ref=dst, send_sem=send.at[index], recv_sem=recv,
            device_id=to, device_id_type=MESH)
        started.append((made, cond))
        if cond is None:
            made.start()
        else:
            pl.when(cond)(made.start)

    def arrived(dst, recv):
        pltpu.make_async_remote_copy(
            src_ref=dst, dst_ref=dst, send_sem=send.at[0], recv_sem=recv,
            device_id=device(x_other, y, c, z), device_id_type=MESH).wait_recv()

    loads = [pltpu.make_async_copy(src, info.at[i], load.at[i])
             for i, src in enumerate((own_h, clu_h, ord_h))]
    loads += [pltpu.make_async_copy(emb_h.at[pl.ds(q * part, part)],
                                    emb.at[pl.ds(q * part, part)], load.at[3 + q])
              for q in range(CHUNKS)]
    for made in loads:
        made.start()

    barrier = pltpu.get_barrier_semaphore()
    for d in range(1, ps):
        pl.semaphore_signal(barrier, inc=1, device_id=plane_device(lax.rem(me + d, ps)),
                            device_id_type=MESH)
    for d in range(1, zs):
        pl.semaphore_signal(barrier, inc=1, device_id=device(x, y, c, lax.rem(z + d, zs)),
                            device_id_type=MESH)

    for made in loads[:3]:
        made.wait()
    low = ((info[0] * 2 + info[1]) * total).astype(jnp.float32)
    key = low + info[2].astype(jnp.float32)
    first = lax.broadcasted_iota(jnp.int32, (8, n), 0) == 0
    meta = jnp.where(first, jnp.broadcast_to(low, (8, n)), jnp.broadcast_to(key, (8, n)))
    meta_p[me] = meta
    meta_z[z] = meta
    for q in range(CHUNKS):
        loads[3 + q].wait()
        e = emb[q * part:(q + 1) * part]
        rows[me, q * part:(q + 1) * part] = (
            e * lax.rsqrt(jnp.sum(e * e, axis=1, keepdims=True) + 1e-6)).astype(jnp.bfloat16)
    pl.semaphore_wait(barrier, ps - 1 + zs - 1)

    def piece(p, h):
        return rows.at[p, pl.ds(h * half, half)]

    def send_piece(p, h, to):
        copy(piece(p, h), piece(p, h), plane_recv.at[p, h], to)

    def wait_piece(p, h):
        arrived(piece(p, h), plane_recv.at[p, h])

    to_x, to_c = device(x_other, y, c, z), device(x, y, c_other, z)

    def slot(s, q):
        return line.at[s, pl.ds(q * part, part)]

    def own(q):
        return rows.at[me, pl.ds(q * part, part)]

    above, below = device(x, y, c, lax.rem(z + 1, zs)), device(x, y, c, lax.rem(z + zs - 1, zs))

    for d in range(1, ps):
        p = lax.rem(me + d, ps)
        copy(meta_p.at[me], meta_p.at[me], meta_recv_p.at[me], plane_device(p))
    for d in range(1, zs):
        to = device(x, y, c, lax.rem(z + d, zs))
        copy(meta_z.at[z], meta_z.at[z], meta_recv_z.at[z], to)
    for q in range(CHUNKS):
        copy(own(q), slot(0, q), up_recv.at[0, q], above, z < mid)
        if downs:
            copy(own(q), slot(ups, q), down_recv.at[0, q], below, z >= mid)
        if q % 2 == 0:
            send_piece(me, q // 2, to_x)
            for d in range(1, ys):
                send_piece(me, 1 - q // 2, device(x, y_peer(d), c, z))
    for h in (0, 1):
        send_piece(me, h, to_c)

    def has_up(t):
        return z > t

    def has_down(t):
        return (z < mid) | (zs - 1 - z > t)

    def step_line(t, q):
        if t < ups:
            @pl.when(has_up(t))
            def _():
                arrived(slot(t, q), up_recv.at[t, q])
            if t + 1 < ups:
                copy(slot(t, q), slot(t + 1, q), up_recv.at[t + 1, q], above, has_up(t) & (z < mid))
            copy(slot(t, q), slot(t, q), up_recv.at[t, q], above,
                 has_up(t) & (z >= mid) & (z < zs - 1))
        if t < downs:
            @pl.when(has_down(t))
            def _():
                arrived(slot(ups + t, q), down_recv.at[t, q])
            if t + 1 < downs:
                copy(slot(ups + t, q), slot(ups + t + 1, q), down_recv.at[t + 1, q], below,
                     has_down(t) & (z >= mid))
            copy(slot(ups + t, q), slot(ups + t, q), down_recv.at[t, q], below, (z > 0) & (z < mid))

    def nth(j):
        k = j // 2
        return place(lax.rem(x + k // ys, 2), lax.rem(y + k, ys), lax.rem(c + j, 2))

    near, every = (0, 2 * (ys + 1)), (0, ps)
    far = (near[1], ps)

    def fold(s):
        return jnp.max(s.reshape(s.shape[0] // 8, 8, s.shape[1]), axis=0)

    def compute(block, origin, start, count, members, both):
        span = pl.ds(start, count)

        def body(j, carry):
            p = nth(j)
            s = lax.dot_general(block[span], rows[p], (((1,), (1,)), ((), ())),
                                preferred_element_type=jnp.float32)
            lo, k, m = col_lo[origin, span], col_key[origin, span], meta_p[p]
            best = col_wide[origin, span]
            parts = []
            for w in range(0, n, 128):
                same = jnp.where(lo == m[0:1, w:w + 128], s[:, w:w + 128], -1.0)
                later = m[1:2, w:w + 128] > k
                if both:
                    best = jnp.maximum(best, jnp.where(later, -1.0, same))
                    parts.append(fold(jnp.where(later, same, -1.0)))
                else:
                    best = jnp.maximum(best, jnp.where(m[1:2, w:w + 128] < k, same, -1.0))
            col_wide[origin, span] = best
            if both:
                row_acc[p] = jnp.maximum(row_acc[p], jnp.concatenate(parts, axis=1))
            return carry

        lax.fori_loop(members[0], members[1], body, 0, unroll=2)

    def compute_own(members):
        compute(rows.at[me], z, 0, n, members, False)

    def compute_up(t, members, start=0, count=n):
        @pl.when(has_up(t) & ((z < mid) | (z == zs - 1)))
        def _():
            compute(line.at[t], jnp.minimum(z, mid) - 1 - t, start, count, members, True)

    def compute_down(t, members):
        if t < downs:
            @pl.when(has_down(t))
            def _():
                compute(line.at[ups + t], jnp.maximum(z + 1, mid) + t, 0, n, members, True)

    def early_plane():
        wait_piece(place(x_other, y, c), 0)
        for d in range(1, ys):
            send_piece(place(x_other, y, c), 0, device(x, y_peer(d), c, z))
        for d in range(1, ys):
            p = place(x, y_peer(d), c)
            wait_piece(p, 1)
            send_piece(p, 1, to_x)
        send_piece(place(x_other, y, c), 0, to_c)
        for d in range(1, ys):
            send_piece(place(x, y_peer(d), c), 1, to_c)

    def late_plane():
        wait_piece(place(x_other, y, c), 1)
        send_piece(place(x_other, y, c), 1, to_c)
        for d in range(1, ys):
            p = place(x, y_peer(d), c)
            wait_piece(p, 0)
            send_piece(p, 0, to_c)
        for j in range(1, near[1], 2):
            for h in (0, 1):
                wait_piece(nth(j), h)

    def far_plane():
        for d in range(1, ys):
            p = place(x_other, y_peer(d), c)
            for h in (0, 1):
                wait_piece(p, h)
                send_piece(p, h, to_c)

    def far_sibling():
        for j in range(far[0] + 1, far[1], 2):
            for h in (0, 1):
                wait_piece(nth(j), h)

    row_acc[...] = jnp.full(row_acc.shape, -1.0, jnp.float32)
    col_wide[...] = jnp.full(col_wide.shape, -1.0, jnp.float32)

    def keys():
        for d in range(1, ps):
            p = lax.rem(me + d, ps)
            arrived(meta_p.at[p], meta_recv_p.at[p])
        for d in range(1, zs):
            o = lax.rem(z + d, zs)
            arrived(meta_z.at[o], meta_recv_z.at[o])
        for o in range(zs):
            m = meta_z[o]
            col_lo[o] = jnp.broadcast_to(m[0:1], (128, n)).T
            col_key[o] = jnp.broadcast_to(m[1:2], (128, n)).T

    last = ups - 1
    for t in range(ups):
        for q in range(CHUNKS):
            step_line(t, q)
            if (t, q) == (0, 1):
                early_plane()
                keys()
            if (t, q) == (0, CHUNKS - 1):
                late_plane()
                compute_own(near)
            if (t, q) == (1, 0):
                compute_up(0, near)
            if (t, q) == (1, 1):
                compute_down(0, near)
            if (t, q) == (1, 2):
                far_plane()
                if last == 1:
                    compute_up(last, near, 0, half)
            if t > 1 and q == 1:
                compute_up(t - 1, every)
                compute_down(t - 1, every)
            if (t, q) == (1, CHUNKS - 1):
                far_sibling()
                compute_own(far)
                compute_up(0, far)
                compute_down(0, far)
                if last == 1:
                    compute_up(last, far, 0, half)
            if last > 1 and (t, q) == (last, 2):
                compute_up(last, every, 0, half)

    def line_home(o):
        return pltpu.make_async_remote_copy(
            src_ref=col_out.at[o], dst_ref=col_in.at[z], send_sem=col_send.at[o],
            recv_sem=col_recv.at[z], device_id=device(x, y, c, o), device_id_type=MESH)

    def finish_line(o, cond):
        @pl.when(cond)
        def _():
            col_out[o] = fold(col_wide[o].T)
            line_home(o).start()

    def plane_home(p):
        return pltpu.make_async_remote_copy(
            src_ref=row_acc.at[p], dst_ref=row_in.at[me], send_sem=row_send.at[p],
            recv_sem=row_recv.at[me], device_id=plane_device(p), device_id_type=MESH)

    for o in range(zs):
        finish_line(o, z != o if o else (z > 0) & (z < zs - 1))
    compute_up(last, every, half, half)
    finish_line(0, z == zs - 1)
    for d in range(1, ps):
        plane_home(lax.rem(me + d, ps)).start()
    best = jnp.maximum(row_acc[me], fold(col_wide[z].T))
    for d in range(1, zs):
        o = lax.rem(z + d, zs)
        arrived(col_in.at[o], col_recv.at[o])
        best = jnp.maximum(best, col_in[o])
    for d in range(1, ps):
        p = lax.rem(me + d, ps)
        arrived(row_in.at[p], row_recv.at[p])
        best = jnp.maximum(best, row_in[p])
    out[...] = jnp.max(best, axis=0, keepdims=True)

    for made, cond in started:
        if cond is None:
            made.wait_send()
        else:
            pl.when(cond)(made.wait_send)
    for d in range(1, zs):
        line_home(lax.rem(z + d, zs)).wait_send()
    for d in range(1, ps):
        plane_home(lax.rem(me + d, ps)).wait_send()


def local(embeddings, owner, cluster, order):
    groups, blocks = lax.axis_size("grp"), lax.axis_size("blk")
    n, width = embeddings.shape
    ys, zs, ps, mid = sizes(groups, blocks)
    slots = mid + max(1, zs - mid - 1)
    f32, bf16 = jnp.float32, jnp.bfloat16
    sends = (ps + zs + CHUNKS * 2 + 4 + 2 * ys + 2 + ys + 3 * ys + 2 * ys
             + 4 * CHUNKS * slots)
    dma = pltpu.SemaphoreType.DMA
    found = pl.pallas_call(
        functools.partial(kernel, groups, blocks),
        out_shape=jax.ShapeDtypeStruct((1, n), f32),
        in_specs=[pl.BlockSpec(memory_space=pltpu.HBM)] * 4,
        out_specs=pl.BlockSpec(memory_space=pltpu.VMEM),
        scratch_shapes=[
            pltpu.VMEM((n, width), f32),
            pltpu.VMEM((3, 1, n), jnp.int32),
            pltpu.VMEM((ps, n, width), bf16),
            pltpu.VMEM((slots, n, width), bf16),
            pltpu.VMEM((ps, 8, n), f32),
            pltpu.VMEM((zs, 8, n), f32),
            pltpu.VMEM((zs, n, 128), f32),
            pltpu.VMEM((zs, n, 128), f32),
            pltpu.VMEM((zs, n, 128), f32),
            pltpu.VMEM((ps, 8, n), f32),
            pltpu.VMEM((zs, 8, n), f32),
            pltpu.VMEM((ps, 8, n), f32),
            pltpu.VMEM((zs, 8, n), f32),
            dma((3 + CHUNKS,)),
            dma((sends,)),
            dma((ps,)),
            dma((zs,)),
            dma((ps, 2)),
            dma((mid, CHUNKS)),
            dma((max(1, zs - mid - 1), CHUNKS)),
            dma((ps,)),
            dma((zs,)),
            dma((ps,)),
            dma((zs,)),
        ],
        compiler_params=pltpu.CompilerParams(
            collective_id=0, has_side_effects=True, vmem_limit_bytes=64 * 1024 * 1024 - 524288),
    )(embeddings, owner.reshape(1, n), cluster.reshape(1, n), order.reshape(1, n))
    return found.reshape(n)


def solution(mesh):
    placed = (
        P(("grp", "blk"), None),
        P(("grp", "blk"), None),
        P(("grp", "blk")),
        P(("grp", "blk")),
    )
    return jax.shard_map(
        local, mesh=mesh, in_specs=placed, out_specs=P(("grp", "blk")), check_vma=False
    )
```

```python
import functools

import jax
import jax.numpy as jnp
from jax import lax
from jax.experimental import pallas as pl
from jax.experimental.pallas import tpu as pltpu
from jax.sharding import PartitionSpec as P

MESH = pl.DeviceIdType.MESH
CHUNKS = 4


def sizes(groups, blocks):
    planes = blocks // 2
    return groups // 2, planes, groups * 2, planes // 2


def kernel(groups, blocks, emb_h, own_h, clu_h, ord_h, out,
           emb, info, rows, line, meta_p, meta_z, col_lo, col_key, col_wide,
           row_acc, col_out, row_in, col_in,
           load, send, meta_recv_p, meta_recv_z, plane_recv, up_recv, down_recv,
           row_send, col_send, row_recv, col_recv):
    n = emb.shape[0]
    half, part = n // 2, n // CHUNKS
    ys, zs, ps, mid = sizes(groups, blocks)
    ups, downs = mid, zs - mid - 1
    total = n * groups * blocks
    g, b = lax.axis_index("grp"), lax.axis_index("blk")
    y, c, z, x = g // 2, g % 2, b // 2, b % 2
    x_other, c_other = 1 - x, 1 - c

    def place(x, y, c):
        return (x * ys + y) * 2 + c

    def device(x, y, c, z):
        return (y * 2 + c, z * 2 + x)

    def plane_device(p):
        return device(p // (2 * ys), (p // 2) % ys, p % 2, z)

    def y_peer(d):
        return lax.rem(y + d, ys)

    me = place(x, y, c)
    used = [0]
    started = []

    def copy(src, dst, recv, to, cond=None):
        index = used[0]
        used[0] += 1
        made = pltpu.make_async_remote_copy(
            src_ref=src, dst_ref=dst, send_sem=send.at[index], recv_sem=recv,
            device_id=to, device_id_type=MESH)
        started.append((made, cond))
        if cond is None:
            made.start()
        else:
            pl.when(cond)(made.start)

    def arrived(dst, recv):
        pltpu.make_async_remote_copy(
            src_ref=dst, dst_ref=dst, send_sem=send.at[0], recv_sem=recv,
            device_id=device(x_other, y, c, z), device_id_type=MESH).wait_recv()

    loads = [pltpu.make_async_copy(src, info.at[i], load.at[i])
             for i, src in enumerate((own_h, clu_h, ord_h))]
    loads += [pltpu.make_async_copy(emb_h.at[pl.ds(q * part, part)],
                                    emb.at[pl.ds(q * part, part)], load.at[3 + q])
              for q in range(CHUNKS)]
    for made in loads:
        made.start()

    barrier = pltpu.get_barrier_semaphore()
    for d in range(1, ps):
        pl.semaphore_signal(barrier, inc=1, device_id=plane_device(lax.rem(me + d, ps)),
                            device_id_type=MESH)
    for d in range(1, zs):
        pl.semaphore_signal(barrier, inc=1, device_id=device(x, y, c, lax.rem(z + d, zs)),
                            device_id_type=MESH)

    for made in loads[:3]:
        made.wait()
    low = ((info[0] * 2 + info[1]) * total).astype(jnp.float32)
    key = low + info[2].astype(jnp.float32)
    first = lax.broadcasted_iota(jnp.int32, (8, n), 0) == 0
    meta = jnp.where(first, jnp.broadcast_to(low, (8, n)), jnp.broadcast_to(key, (8, n)))
    meta_p[me] = meta
    meta_z[z] = meta
    for q in range(CHUNKS):
        loads[3 + q].wait()
        e = emb[q * part:(q + 1) * part]
        rows[me, q * part:(q + 1) * part] = (
            e * lax.rsqrt(jnp.sum(e * e, axis=1, keepdims=True) + 1e-6)).astype(jnp.bfloat16)
    pl.semaphore_wait(barrier, ps - 1 + zs - 1)

    def piece(p, h):
        return rows.at[p, pl.ds(h * half, half)]

    def send_piece(p, h, to):
        copy(piece(p, h), piece(p, h), plane_recv.at[p, h], to)

    def wait_piece(p, h):
        arrived(piece(p, h), plane_recv.at[p, h])

    to_x, to_c = device(x_other, y, c, z), device(x, y, c_other, z)

    def slot(s, q):
        return line.at[s, pl.ds(q * part, part)]

    def own(q):
        return rows.at[me, pl.ds(q * part, part)]

    above, below = device(x, y, c, lax.rem(z + 1, zs)), device(x, y, c, lax.rem(z + zs - 1, zs))

    for d in range(1, ps):
        p = lax.rem(me + d, ps)
        copy(meta_p.at[me], meta_p.at[me], meta_recv_p.at[me], plane_device(p))
    for d in range(1, zs):
        to = device(x, y, c, lax.rem(z + d, zs))
        copy(meta_z.at[z], meta_z.at[z], meta_recv_z.at[z], to)
    for q in range(CHUNKS):
        copy(own(q), slot(0, q), up_recv.at[0, q], above, z < mid)
        if downs:
            copy(own(q), slot(ups, q), down_recv.at[0, q], below, z >= mid)
    def send_own(hx, hy):
        send_piece(me, hx, to_x)
        for d in range(1, ys):
            send_piece(me, hy, device(x, y_peer(d), c, z))

    send_own(0, 1)

    def has_up(t):
        return z > t

    def has_down(t):
        return (z < mid) | (zs - 1 - z > t)

    def step_line(t, q):
        if t < ups:
            @pl.when(has_up(t))
            def _():
                arrived(slot(t, q), up_recv.at[t, q])
            if t + 1 < ups:
                copy(slot(t, q), slot(t + 1, q), up_recv.at[t + 1, q], above, has_up(t) & (z < mid))
            copy(slot(t, q), slot(t, q), up_recv.at[t, q], above,
                 has_up(t) & (z >= mid) & (z < zs - 1))
        if t < downs:
            @pl.when(has_down(t))
            def _():
                arrived(slot(ups + t, q), down_recv.at[t, q])
            if t + 1 < downs:
                copy(slot(ups + t, q), slot(ups + t + 1, q), down_recv.at[t + 1, q], below,
                     has_down(t) & (z >= mid))
            copy(slot(ups + t, q), slot(ups + t, q), down_recv.at[t, q], below, (z > 0) & (z < mid))

    def nth(j):
        k = j // 2
        return place(lax.rem(x + k // ys, 2), lax.rem(y + k, ys), lax.rem(c + j, 2))

    near, every = (0, 2 * (ys + 1)), (0, ps)
    far = (near[1], ps)

    def fold(s):
        return jnp.max(s.reshape(s.shape[0] // 8, 8, s.shape[1]), axis=0)

    def compute(block, origin, start, count, members, both):
        span = pl.ds(start, count)

        def body(j, carry):
            p = nth(j)
            s = lax.dot_general(block[span], rows[p], (((1,), (1,)), ((), ())),
                                preferred_element_type=jnp.float32)
            lo, k, m = col_lo[origin, span], col_key[origin, span], meta_p[p]
            best = col_wide[origin, span]
            parts = []
            for w in range(0, n, 128):
                same = jnp.where(lo == m[0:1, w:w + 128], s[:, w:w + 128], -1.0)
                later = m[1:2, w:w + 128] > k
                if both:
                    best = jnp.maximum(best, jnp.where(later, -1.0, same))
                    parts.append(fold(jnp.where(later, same, -1.0)))
                else:
                    best = jnp.maximum(best, jnp.where(m[1:2, w:w + 128] < k, same, -1.0))
            col_wide[origin, span] = best
            if both:
                row_acc[p] = jnp.maximum(row_acc[p], jnp.concatenate(parts, axis=1))
            return carry

        lax.fori_loop(members[0], members[1], body, 0, unroll=2)

    def compute_own(members):
        compute(rows.at[me], z, 0, n, members, False)

    def compute_up(t, members, start=0, count=n):
        @pl.when(has_up(t) & ((z < mid) | (z == zs - 1)))
        def _():
            compute(line.at[t], jnp.minimum(z, mid) - 1 - t, start, count, members, True)

    def compute_down(t, members):
        if t < downs:
            @pl.when(has_down(t))
            def _():
                compute(line.at[ups + t], jnp.maximum(z + 1, mid) + t, 0, n, members, True)

    def early_plane():
        wait_piece(place(x_other, y, c), 0)
        for d in range(1, ys):
            send_piece(place(x_other, y, c), 0, device(x, y_peer(d), c, z))
        for d in range(1, ys):
            p = place(x, y_peer(d), c)
            wait_piece(p, 1)
            send_piece(p, 1, to_x)
        send_piece(place(x_other, y, c), 0, to_c)
        for d in range(1, ys):
            send_piece(place(x, y_peer(d), c), 1, to_c)

    def late_plane():
        wait_piece(place(x_other, y, c), 1)
        send_piece(place(x_other, y, c), 1, to_c)
        for d in range(1, ys):
            p = place(x, y_peer(d), c)
            wait_piece(p, 0)
            send_piece(p, 0, to_c)
        for j in range(1, near[1], 2):
            for h in (0, 1):
                wait_piece(nth(j), h)

    def far_plane():
        for d in range(1, ys):
            p = place(x_other, y_peer(d), c)
            for h in (0, 1):
                wait_piece(p, h)
                send_piece(p, h, to_c)

    def far_sibling():
        for j in range(far[0] + 1, far[1], 2):
            for h in (0, 1):
                wait_piece(nth(j), h)

    row_acc[...] = jnp.full(row_acc.shape, -1.0, jnp.float32)
    col_wide[...] = jnp.full(col_wide.shape, -1.0, jnp.float32)

    def keys():
        for d in range(1, ps):
            p = lax.rem(me + d, ps)
            arrived(meta_p.at[p], meta_recv_p.at[p])
        for d in range(1, zs):
            o = lax.rem(z + d, zs)
            arrived(meta_z.at[o], meta_recv_z.at[o])
        for o in range(zs):
            m = meta_z[o]
            col_lo[o] = jnp.broadcast_to(m[0:1], (128, n)).T
            col_key[o] = jnp.broadcast_to(m[1:2], (128, n)).T

    last = ups - 1
    for t in range(ups):
        for q in range(CHUNKS):
            step_line(t, q)
            if (t, q) == (0, 1):
                send_own(1, 0)
                early_plane()
                for h in (0, 1):
                    send_piece(me, h, to_c)
                keys()
            if (t, q) == (0, CHUNKS - 1):
                late_plane()
                compute_own(near)
            if (t, q) == (1, 0):
                compute_up(0, near)
            if (t, q) == (1, 1):
                far_plane()
                compute_down(0, near)
            if (t, q) == (1, 2):
                far_sibling()
                compute_own(far)
                compute_up(0, far)
                compute_down(0, far)
            if t > 1 and q == 1:
                compute_up(t - 1, every)
                compute_down(t - 1, every)
            if (t, q) == (last, 2):
                compute_up(last, every, 0, half)

    def line_home(o):
        return pltpu.make_async_remote_copy(
            src_ref=col_out.at[o], dst_ref=col_in.at[z], send_sem=col_send.at[o],
            recv_sem=col_recv.at[z], device_id=device(x, y, c, o), device_id_type=MESH)

    def finish_line(o, cond):
        @pl.when(cond)
        def _():
            col_out[o] = fold(col_wide[o].T)
            line_home(o).start()

    def plane_home(p):
        return pltpu.make_async_remote_copy(
            src_ref=row_acc.at[p], dst_ref=row_in.at[me], send_sem=row_send.at[p],
            recv_sem=row_recv.at[me], device_id=plane_device(p), device_id_type=MESH)

    for o in range(zs):
        finish_line(o, z != o if o else (z > 0) & (z < zs - 1))
    compute_up(last, every, half, half)
    finish_line(0, z == zs - 1)
    for d in range(1, ps):
        plane_home(lax.rem(me + d, ps)).start()
    best = jnp.maximum(row_acc[me], fold(col_wide[z].T))
    for d in range(1, zs):
        o = lax.rem(z + d, zs)
        arrived(col_in.at[o], col_recv.at[o])
        best = jnp.maximum(best, col_in[o])
    for d in range(1, ps):
        p = lax.rem(me + d, ps)
        arrived(row_in.at[p], row_recv.at[p])
        best = jnp.maximum(best, row_in[p])
    out[...] = best

    for made, cond in started:
        if cond is None:
            made.wait_send()
        else:
            pl.when(cond)(made.wait_send)
    for d in range(1, zs):
        line_home(lax.rem(z + d, zs)).wait_send()
    for d in range(1, ps):
        plane_home(lax.rem(me + d, ps)).wait_send()


def local(embeddings, owner, cluster, order):
    groups, blocks = lax.axis_size("grp"), lax.axis_size("blk")
    n, width = embeddings.shape
    ys, zs, ps, mid = sizes(groups, blocks)
    slots = mid + max(1, zs - mid - 1)
    f32, bf16 = jnp.float32, jnp.bfloat16
    sends = (ps + zs + CHUNKS * 2 + 4 + 2 * ys + 2 + ys + 3 * ys + 2 * ys
             + 4 * CHUNKS * slots)
    dma = pltpu.SemaphoreType.DMA
    found = pl.pallas_call(
        functools.partial(kernel, groups, blocks),
        out_shape=jax.ShapeDtypeStruct((8, n), f32),
        in_specs=[pl.BlockSpec(memory_space=pltpu.HBM)] * 4,
        out_specs=pl.BlockSpec(memory_space=pltpu.VMEM),
        scratch_shapes=[
            pltpu.VMEM((n, width), f32),
            pltpu.VMEM((3, 1, n), jnp.int32),
            pltpu.VMEM((ps, n, width), bf16),
            pltpu.VMEM((slots, n, width), bf16),
            pltpu.VMEM((ps, 8, n), f32),
            pltpu.VMEM((zs, 8, n), f32),
            pltpu.VMEM((zs, n, 128), f32),
            pltpu.VMEM((zs, n, 128), f32),
            pltpu.VMEM((zs, n, 128), f32),
            pltpu.VMEM((ps, 8, n), f32),
            pltpu.VMEM((zs, 8, n), f32),
            pltpu.VMEM((ps, 8, n), f32),
            pltpu.VMEM((zs, 8, n), f32),
            dma((3 + CHUNKS,)),
            dma((sends,)),
            dma((ps,)),
            dma((zs,)),
            dma((ps, 2)),
            dma((mid, CHUNKS)),
            dma((max(1, zs - mid - 1), CHUNKS)),
            dma((ps,)),
            dma((zs,)),
            dma((ps,)),
            dma((zs,)),
        ],
        compiler_params=pltpu.CompilerParams(
            collective_id=0, has_side_effects=True, vmem_limit_bytes=64 * 1024 * 1024 - 524288),
    )(embeddings, owner.reshape(1, n), cluster.reshape(1, n), order.reshape(1, n))
    return jnp.max(found, axis=0)


def solution(mesh):
    placed = (
        P(("grp", "blk"), None),
        P(("grp", "blk"), None),
        P(("grp", "blk")),
        P(("grp", "blk")),
    )
    return jax.shard_map(
        local, mesh=mesh, in_specs=placed, out_specs=P(("grp", "blk")), check_vma=False
    )
```

```python
import functools

import jax
import jax.numpy as jnp
from jax import lax
from jax.experimental import pallas as pl
from jax.experimental.pallas import tpu as pltpu
from jax.sharding import PartitionSpec as P

MESH = pl.DeviceIdType.MESH
CHUNKS = 4


def sizes(groups, blocks):
    planes = blocks // 2
    return groups // 2, planes, groups * 2, planes // 2


def kernel(groups, blocks, emb_h, own_h, clu_h, ord_h, out,
           emb, info, rows, line, meta_p, meta_z, col_lo, col_key, col_wide,
           row_acc, col_out, row_in, col_in,
           load, send, meta_recv_p, meta_recv_z, plane_recv, up_recv, down_recv,
           row_send, col_send, row_recv, col_recv):
    n = emb.shape[0]
    half, part = n // 2, n // CHUNKS
    ys, zs, ps, mid = sizes(groups, blocks)
    ups, downs = mid, zs - mid - 1
    total = n * groups * blocks
    g, b = lax.axis_index("grp"), lax.axis_index("blk")
    y, c, z, x = g // 2, g % 2, b // 2, b % 2
    x_other, c_other = 1 - x, 1 - c

    def place(x, y, c):
        return (x * ys + y) * 2 + c

    def device(x, y, c, z):
        return (y * 2 + c, z * 2 + x)

    def plane_device(p):
        return device(p // (2 * ys), (p // 2) % ys, p % 2, z)

    def y_peer(d):
        return lax.rem(y + d, ys)

    me = place(x, y, c)
    used = [0]
    started = []

    def copy(src, dst, recv, to, cond=None):
        index = used[0]
        used[0] += 1
        made = pltpu.make_async_remote_copy(
            src_ref=src, dst_ref=dst, send_sem=send.at[index], recv_sem=recv,
            device_id=to, device_id_type=MESH)
        started.append((made, cond))
        if cond is None:
            made.start()
        else:
            pl.when(cond)(made.start)

    def arrived(dst, recv):
        pltpu.make_async_remote_copy(
            src_ref=dst, dst_ref=dst, send_sem=send.at[0], recv_sem=recv,
            device_id=device(x_other, y, c, z), device_id_type=MESH).wait_recv()

    loads = [pltpu.make_async_copy(src, info.at[i], load.at[i])
             for i, src in enumerate((own_h, clu_h, ord_h))]
    loads += [pltpu.make_async_copy(emb_h.at[pl.ds(q * part, part)],
                                    emb.at[pl.ds(q * part, part)], load.at[3 + q])
              for q in range(CHUNKS)]
    for made in loads:
        made.start()

    barrier = pltpu.get_barrier_semaphore()
    for d in range(1, ps):
        pl.semaphore_signal(barrier, inc=1, device_id=plane_device(lax.rem(me + d, ps)),
                            device_id_type=MESH)
    for d in range(1, zs):
        pl.semaphore_signal(barrier, inc=1, device_id=device(x, y, c, lax.rem(z + d, zs)),
                            device_id_type=MESH)

    for made in loads[:3]:
        made.wait()
    low = ((info[0] * 2 + info[1]) * total).astype(jnp.float32)
    key = low + info[2].astype(jnp.float32)
    first = lax.broadcasted_iota(jnp.int32, (8, n), 0) == 0
    meta = jnp.where(first, jnp.broadcast_to(low, (8, n)), jnp.broadcast_to(key, (8, n)))
    meta_p[me] = meta
    meta_z[z] = meta
    for q in range(CHUNKS):
        loads[3 + q].wait()
        e = emb[q * part:(q + 1) * part]
        rows[me, q * part:(q + 1) * part] = (
            e * lax.rsqrt(jnp.sum(e * e, axis=1, keepdims=True) + 1e-6)).astype(jnp.bfloat16)
    pl.semaphore_wait(barrier, ps - 1 + zs - 1)

    def piece(p, h):
        return rows.at[p, pl.ds(h * half, half)]

    def send_piece(p, h, to):
        copy(piece(p, h), piece(p, h), plane_recv.at[p, h], to)

    def wait_piece(p, h):
        arrived(piece(p, h), plane_recv.at[p, h])

    to_x, to_c = device(x_other, y, c, z), device(x, y, c_other, z)

    def slot(s, q):
        return line.at[s, pl.ds(q * part, part)]

    def own(q):
        return rows.at[me, pl.ds(q * part, part)]

    above, below = device(x, y, c, lax.rem(z + 1, zs)), device(x, y, c, lax.rem(z + zs - 1, zs))

    for d in range(1, ps):
        p = lax.rem(me + d, ps)
        copy(meta_p.at[me], meta_p.at[me], meta_recv_p.at[me], plane_device(p))
    for d in range(1, zs):
        to = device(x, y, c, lax.rem(z + d, zs))
        copy(meta_z.at[z], meta_z.at[z], meta_recv_z.at[z], to)
    for q in range(CHUNKS):
        copy(own(q), slot(0, q), up_recv.at[0, q], above, z < mid)
        if downs:
            copy(own(q), slot(ups, q), down_recv.at[0, q], below, z >= mid)
    for hx, hy in ((0, 1), (1, 0)):
        send_piece(me, hx, to_x)
        for d in range(1, ys):
            send_piece(me, hy, device(x, y_peer(d), c, z))
    for h in (0, 1):
        send_piece(me, h, to_c)

    def has_up(t):
        return z > t

    def has_down(t):
        return (z < mid) | (zs - 1 - z > t)

    def step_line(t, q):
        if t < ups:
            @pl.when(has_up(t))
            def _():
                arrived(slot(t, q), up_recv.at[t, q])
            if t + 1 < ups:
                copy(slot(t, q), slot(t + 1, q), up_recv.at[t + 1, q], above, has_up(t) & (z < mid))
            copy(slot(t, q), slot(t, q), up_recv.at[t, q], above,
                 has_up(t) & (z >= mid) & (z < zs - 1))
        if t < downs:
            @pl.when(has_down(t))
            def _():
                arrived(slot(ups + t, q), down_recv.at[t, q])
            if t + 1 < downs:
                copy(slot(ups + t, q), slot(ups + t + 1, q), down_recv.at[t + 1, q], below,
                     has_down(t) & (z >= mid))
            copy(slot(ups + t, q), slot(ups + t, q), down_recv.at[t, q], below, (z > 0) & (z < mid))

    def nth(j):
        k = j // 2
        return place(lax.rem(x + k // ys, 2), lax.rem(y + k, ys), lax.rem(c + j, 2))

    near, every = (0, 2 * (ys + 1)), (0, ps)
    far = (near[1], ps)

    def fold(s):
        return jnp.max(s.reshape(s.shape[0] // 8, 8, s.shape[1]), axis=0)

    def compute(block, origin, start, count, members, both):
        span = pl.ds(start, count)

        def body(j, carry):
            p = nth(j)
            s = lax.dot_general(block[span], rows[p], (((1,), (1,)), ((), ())),
                                preferred_element_type=jnp.float32)
            lo, k, m = col_lo[origin, span], col_key[origin, span], meta_p[p]
            best = col_wide[origin, span]
            parts = []
            for w in range(0, n, 128):
                same = jnp.where(lo == m[0:1, w:w + 128], s[:, w:w + 128], -1.0)
                later = m[1:2, w:w + 128] > k
                if both:
                    best = jnp.maximum(best, jnp.where(later, -1.0, same))
                    parts.append(fold(jnp.where(later, same, -1.0)))
                else:
                    best = jnp.maximum(best, jnp.where(m[1:2, w:w + 128] < k, same, -1.0))
            col_wide[origin, span] = best
            if both:
                row_acc[p] = jnp.maximum(row_acc[p], jnp.concatenate(parts, axis=1))
            return carry

        lax.fori_loop(members[0], members[1], body, 0, unroll=2)

    def compute_own(members):
        compute(rows.at[me], z, 0, n, members, False)

    def compute_up(t, members, start=0, count=n):
        @pl.when(has_up(t) & ((z < mid) | (z == zs - 1)))
        def _():
            compute(line.at[t], jnp.minimum(z, mid) - 1 - t, start, count, members, True)

    def compute_down(t, members):
        if t < downs:
            @pl.when(has_down(t))
            def _():
                compute(line.at[ups + t], jnp.maximum(z + 1, mid) + t, 0, n, members, True)

    def early_plane():
        wait_piece(place(x_other, y, c), 0)
        for d in range(1, ys):
            send_piece(place(x_other, y, c), 0, device(x, y_peer(d), c, z))
        for d in range(1, ys):
            p = place(x, y_peer(d), c)
            wait_piece(p, 1)
            send_piece(p, 1, to_x)
        send_piece(place(x_other, y, c), 0, to_c)
        for d in range(1, ys):
            send_piece(place(x, y_peer(d), c), 1, to_c)

    def late_plane():
        wait_piece(place(x_other, y, c), 1)
        send_piece(place(x_other, y, c), 1, to_c)
        for d in range(1, ys):
            p = place(x, y_peer(d), c)
            wait_piece(p, 0)
            send_piece(p, 0, to_c)
        for j in range(1, near[1], 2):
            for h in (0, 1):
                wait_piece(nth(j), h)

    def far_plane():
        for d in range(1, ys):
            p = place(x_other, y_peer(d), c)
            for h in (0, 1):
                wait_piece(p, h)
                send_piece(p, h, to_c)

    def far_sibling():
        for j in range(far[0] + 1, far[1], 2):
            for h in (0, 1):
                wait_piece(nth(j), h)

    row_acc[...] = jnp.full(row_acc.shape, -1.0, jnp.float32)
    col_wide[...] = jnp.full(col_wide.shape, -1.0, jnp.float32)

    def keys():
        for d in range(1, ps):
            p = lax.rem(me + d, ps)
            arrived(meta_p.at[p], meta_recv_p.at[p])
        for d in range(1, zs):
            o = lax.rem(z + d, zs)
            arrived(meta_z.at[o], meta_recv_z.at[o])
        for o in range(zs):
            m = meta_z[o]
            col_lo[o] = jnp.broadcast_to(m[0:1], (128, n)).T
            col_key[o] = jnp.broadcast_to(m[1:2], (128, n)).T

    last = ups - 1
    for t in range(ups):
        for q in range(CHUNKS):
            step_line(t, q)
            if (t, q) == (0, 1):
                early_plane()
                keys()
            if (t, q) == (0, CHUNKS - 1):
                late_plane()
                compute_own(near)
            if (t, q) == (1, 0):
                compute_up(0, near)
            if (t, q) == (1, 1):
                compute_down(0, near)
            if (t, q) == (1, 2) and last == 1:
                compute_up(last, near, 0, half)
            if (t, q) == (1, CHUNKS - 1):
                far_plane()
                if last == 1:
                    compute_up(last, near, half, half)
                far_sibling()
                compute_own(far)
                compute_up(0, far)
                compute_down(0, far)
            if t > 1 and q == 1:
                compute_up(t - 1, every)
                compute_down(t - 1, every)
            if (t, q) == (last, 2) and last > 1:
                compute_up(last, every, 0, half)

    def line_home(o):
        return pltpu.make_async_remote_copy(
            src_ref=col_out.at[o], dst_ref=col_in.at[z], send_sem=col_send.at[o],
            recv_sem=col_recv.at[z], device_id=device(x, y, c, o), device_id_type=MESH)

    def finish_line(o, cond):
        @pl.when(cond)
        def _():
            col_out[o] = fold(col_wide[o].T)
            line_home(o).start()

    def plane_home(p):
        return pltpu.make_async_remote_copy(
            src_ref=row_acc.at[p], dst_ref=row_in.at[me], send_sem=row_send.at[p],
            recv_sem=row_recv.at[me], device_id=plane_device(p), device_id_type=MESH)

    for o in range(zs):
        finish_line(o, z != o if o else (z > 0) & (z < zs - 1))
    if last > 1:
        compute_up(last, every, half, half)
    else:
        compute_up(last, far)
    finish_line(0, z == zs - 1)
    for d in range(1, ps):
        plane_home(lax.rem(me + d, ps)).start()
    best = jnp.maximum(row_acc[me], fold(col_wide[z].T))
    for d in range(1, zs):
        o = lax.rem(z + d, zs)
        arrived(col_in.at[o], col_recv.at[o])
        best = jnp.maximum(best, col_in[o])
    for d in range(1, ps):
        p = lax.rem(me + d, ps)
        arrived(row_in.at[p], row_recv.at[p])
        best = jnp.maximum(best, row_in[p])
    out[...] = jnp.max(best, axis=0, keepdims=True)

    for made, cond in started:
        if cond is None:
            made.wait_send()
        else:
            pl.when(cond)(made.wait_send)
    for d in range(1, zs):
        line_home(lax.rem(z + d, zs)).wait_send()
    for d in range(1, ps):
        plane_home(lax.rem(me + d, ps)).wait_send()


def local(embeddings, owner, cluster, order):
    groups, blocks = lax.axis_size("grp"), lax.axis_size("blk")
    n, width = embeddings.shape
    ys, zs, ps, mid = sizes(groups, blocks)
    slots = mid + max(1, zs - mid - 1)
    f32, bf16 = jnp.float32, jnp.bfloat16
    sends = (ps + zs + CHUNKS * 2 + 4 + 2 * ys + 2 + ys + 3 * ys + 2 * ys
             + 4 * CHUNKS * slots)
    dma = pltpu.SemaphoreType.DMA
    found = pl.pallas_call(
        functools.partial(kernel, groups, blocks),
        out_shape=jax.ShapeDtypeStruct((1, n), f32),
        in_specs=[pl.BlockSpec(memory_space=pltpu.HBM)] * 4,
        out_specs=pl.BlockSpec(memory_space=pltpu.VMEM),
        scratch_shapes=[
            pltpu.VMEM((n, width), f32),
            pltpu.VMEM((3, 1, n), jnp.int32),
            pltpu.VMEM((ps, n, width), bf16),
            pltpu.VMEM((slots, n, width), bf16),
            pltpu.VMEM((ps, 8, n), f32),
            pltpu.VMEM((zs, 8, n), f32),
            pltpu.VMEM((zs, n, 128), f32),
            pltpu.VMEM((zs, n, 128), f32),
            pltpu.VMEM((zs, n, 128), f32),
            pltpu.VMEM((ps, 8, n), f32),
            pltpu.VMEM((zs, 8, n), f32),
            pltpu.VMEM((ps, 8, n), f32),
            pltpu.VMEM((zs, 8, n), f32),
            dma((3 + CHUNKS,)),
            dma((sends,)),
            dma((ps,)),
            dma((zs,)),
            dma((ps, 2)),
            dma((mid, CHUNKS)),
            dma((max(1, zs - mid - 1), CHUNKS)),
            dma((ps,)),
            dma((zs,)),
            dma((ps,)),
            dma((zs,)),
        ],
        compiler_params=pltpu.CompilerParams(
            collective_id=0, has_side_effects=True, vmem_limit_bytes=64 * 1024 * 1024 - 524288),
    )(embeddings, owner.reshape(1, n), cluster.reshape(1, n), order.reshape(1, n))
    return found.reshape(n)


def solution(mesh):
    placed = (
        P(("grp", "blk"), None),
        P(("grp", "blk"), None),
        P(("grp", "blk")),
        P(("grp", "blk")),
    )
    return jax.shard_map(
        local, mesh=mesh, in_specs=placed, out_specs=P(("grp", "blk")), check_vma=False
    )
```
